128 devices in a mesh: dp: 8 (over z, core), seq: 16 (over x, y).
Axes of the slice: x: 4, y: 4, z: 4, core: 2. Of those that a mesh axis runs over, the one named last changes fastest.
Arguments:
- tokens: bfloat16 [8, 2048, 1024], P('dp', 'seq'), may hold values from -6 to 6
- w_qkv: bfloat16 [1024, 2048], P(('dp', 'seq')), may hold values from -0.1875 to 0.1875
- w_out: bfloat16 [1024, 1024], P(('dp', 'seq')), may hold values from -1 to 1
- w_gu: bfloat16 [1024, 9216], P(('dp', 'seq')), may hold values from -0.1875 to 0.1875
- w_down: bfloat16 [1024, 4608], P(('dp', 'seq')), may hold values from -0.125 to 0.125
- gains: bfloat16 [2176], P(('dp', 'seq')), may hold values from 0.5 to 1.5
- span_order: int32 [8, 32], P('dp'), may hold values from 0 to 31, as said below
- d_out: bfloat16 [8, 2048, 1024], P('dp', 'seq'), may hold values from -6 to 6
Outputs:
- result: bfloat16 [8, 2048, 1024], P('dp', 'seq')
- d_tokens: float32 [8, 2048, 1024], P('dp', 'seq')
- g_qkv: float32 [1024, 2048], P(('dp', 'seq'))
- g_out: float32 [1024, 1024], P(('dp', 'seq'))
- g_gu: float32 [1024, 9216], P(('dp', 'seq'))
- g_down: float32 [1024, 4608], P(('dp', 'seq'))
- g_gains: float32 [2176], P(('dp', 'seq'))
The draws below stay inside these ranges and needn't reach their ends.
Inputs may be any that keep to these rules, and one draw needn't show every extreme that they name: `span_order`: each row is a permutation of the 32 spans; slots 2 i and 2 i + 1 hold spans c and 31 - c for some c.
All inputs are finite; a program needn't handle non-finite values.
Results may differ from the reference program's by a relative error of at most 0.02.
Values may be sent and summed in bfloat16 or wider, within the bound.
No kernel may reach another device: no remote copies, remote signals or barrier semaphores. Data moves between devices by JAX's collectives and lax.ppermute only.
A program may use at most 192 MiB of HBM per device.

```python
import jax
import jax.numpy as jnp
from jax import lax

D = 1024
H = 16
KVH = 8
HD = 64
FF = 4608
LOC = 128
SPANS = 32
LENGTH = 2048
SEQS = 8
QKV = 2048
GAINS = 2176


def draw_span_order(key, part):
    key = jax.random.fold_in(key, 7)
    pairs_count = SPANS // 2
    first_key, second_key = jax.random.split(key)
    row_keys = jax.random.split(first_key, SEQS)
    pairs = jax.vmap(lambda k: jax.random.permutation(k, pairs_count))(row_keys)
    flips = jax.random.randint(second_key, (SEQS, pairs_count), 0, 2)
    leading = jnp.where(flips == 1, SPANS - 1 - pairs, pairs)
    trailing = SPANS - 1 - leading
    return jnp.stack([leading, trailing], axis=-1).reshape(SEQS, SPANS).astype(jnp.int32)


def steps_of(stream_key, dims, cuts, least, high):
    def one(position, parts):
        heights = jax.random.uniform(jax.random.fold_in(jax.random.fold_in(stream_key, 6), position), (parts,), jnp.float32, least / len(cuts), high / len(cuts))
        return jnp.repeat(jnp.exp(heights), dims[position] // parts).reshape((-1,) + (1,) * (len(dims) - position - 1))

    level = one(*cuts[0])
    for cut in cuts[1:]:
        level = level * one(*cut)
    return level


def scatter_about(rng, dims, spread, limit, shards=(), kind=jnp.bfloat16):
    drawn = spread * jax.random.normal(rng, dims, jnp.float32)
    if shards:
        drawn = drawn * steps_of(rng, dims, shards, -0.22, 0.18)
    return jnp.clip(drawn, -limit, limit).astype(kind)


def setup_inputs(seed: int = 0) -> dict:
    key_list = jax.random.split(jax.random.key(seed), 9)
    tokens = scatter_about(key_list[0], (SEQS, LENGTH, D), 1.0, 6.0, ((0, 8), (1, 16)))
    w_qkv = scatter_about(key_list[1], (D, QKV), D ** -0.5, 0.1875, ((0, 128),))
    w_out = scatter_about(key_list[2], (D, D), (D // 32) ** -0.5, 1.0, ((0, 128),))
    w_gu = scatter_about(key_list[3], (D, 2 * FF), D ** -0.5, 0.1875, ((0, 128),))
    w_down = scatter_about(key_list[4], (D, FF), (FF // 2) ** -0.5, 0.125, ((0, 128),))
    gains = jnp.clip(1.0 + 0.1 * jax.random.normal(key_list[5], (GAINS,), jnp.float32), 0.5, 1.5).astype(jnp.bfloat16)
    span_order = draw_span_order(jax.random.fold_in(key_list[8], 71), 0)
    d_out = scatter_about(key_list[7], (SEQS, LENGTH, D), 1.0, 6.0, ((0, 8), (1, 16)))
    return dict(tokens=tokens, w_qkv=w_qkv, w_out=w_out, w_gu=w_gu, w_down=w_down, gains=gains, span_order=span_order, d_out=d_out)


EPSILON = 1e-05
THETA = 1000000.0

@jax.custom_vjp
def low(v):
    return lax.optimization_barrier(v.astype(jnp.bfloat16)).astype(jnp.float32)

@jax.custom_vjp
def low_back(v):
    return v

def low_keep(v):
    return (low(v), None)

def low_pass(kept, grad):
    return (grad,)

def back_keep(v):
    return (v, None)

def back_low(kept, grad):
    return (low(grad),)
low.defvjp(low_keep, low_pass)
low_back.defvjp(back_keep, back_low)

def normed(values, gain):
    return values * lax.rsqrt(lax.optimization_barrier(jnp.mean(values * values, axis=-1, keepdims=True)) + EPSILON) * gain

def rotate(values, positions):
    half = HD // 2
    freqs = THETA ** (-(jnp.arange(half, dtype=jnp.float32) * 2.0 / HD))
    turned = positions.astype(jnp.float32)[:, None] * freqs[None, :]
    cosine = jnp.cos(turned)[:, None, :]
    sine = jnp.sin(turned)[:, None, :]
    first = values[..., :half]
    second = values[..., half:]
    return jnp.concatenate([first * cosine - second * sine, second * cosine + first * sine], axis=-1)

def attend(queries, keys, values, positions):
    group = H // KVH
    keys = jnp.repeat(keys, group, axis=1)
    values = jnp.repeat(values, group, axis=1)
    block = 512 if LENGTH % 512 == 0 else LENGTH

    def one_block(start):
        q_part = lax.dynamic_slice_in_dim(queries, start, block, 0)
        p_part = lax.dynamic_slice_in_dim(positions, start, block, 0)
        scores = low_back(jnp.einsum('qhd,khd->hqk', q_part, keys, precision=lax.Precision.HIGHEST) * HD ** (-0.5))
        scores = jnp.where(p_part[None, :, None] >= positions[None, None, :], scores, -1e+30)
        top = lax.optimization_barrier(jnp.max(scores, axis=-1, keepdims=True))
        weights = jnp.exp(scores - top)
        probs = weights / lax.optimization_barrier(jnp.sum(weights, axis=-1, keepdims=True))
        return jnp.einsum('hqk,khd->qhd', low(probs), values, precision=lax.Precision.HIGHEST)
    starts = jnp.arange(LENGTH // block, dtype=jnp.int32) * block
    outs = lax.map(jax.checkpoint(one_block), starts)
    return outs.reshape(LENGTH, H * HD)

def forward(inputs, w_qkv, w_out, w_gu, w_down, gains, positions):
    a_gain = gains[:D]
    f_gain = gains[D:2 * D]
    q_gain = gains[2 * D:2 * D + HD]
    k_gain = gains[2 * D + HD:]
    hidden = low(normed(inputs, a_gain))
    mixed = low_back(jnp.dot(hidden, w_qkv, precision=lax.Precision.HIGHEST))
    kv_width = KVH * HD
    q_raw = mixed[:, :D].reshape(LENGTH, H, HD)
    k_raw = mixed[:, D:D + kv_width].reshape(LENGTH, KVH, HD)
    v_raw = mixed[:, D + kv_width:].reshape(LENGTH, KVH, HD)
    queries = low(rotate(normed(q_raw, q_gain), positions))
    keys = low(rotate(normed(k_raw, k_gain), positions))
    values = low(v_raw)
    attended = low_back(low(attend(queries, keys, values, positions)))
    middle = inputs + low_back(jnp.dot(attended, w_out, precision=lax.Precision.HIGHEST))
    hidden_two = low(normed(middle, f_gain))
    gate_up = low_back(jnp.dot(hidden_two, w_gu, precision=lax.Precision.HIGHEST))
    activated = low_back(low(jax.nn.silu(gate_up[:, :FF]) * gate_up[:, FF:]))
    return middle + jnp.dot(activated, w_down.T, precision=lax.Precision.HIGHEST)

def reference(tokens, w_qkv, w_out, w_gu, w_down, gains, span_order, d_out):
    weights = tuple((a.astype(jnp.float32) for a in (w_qkv, w_out, w_gu, w_down, gains)))
    half_span = LOC // 2
    spots = jnp.arange(LENGTH, dtype=jnp.int32)

    def one(carry, item):
        inputs, order, cotangent = item
        positions = (order[spots // half_span] * half_span + spots % half_span).astype(jnp.int32)
        outputs, pull = jax.vjp(lambda xin, wa, wb, wc, wd, wg: forward(xin, wa, wb, wc, wd, wg, positions), inputs.astype(jnp.float32), *weights)
        grads = pull(cotangent.astype(jnp.float32))
        summed = tuple((c + g for c, g in zip(carry, grads[1:])))
        return (summed, (outputs.astype(jnp.bfloat16), grads[0]))
    start = tuple((jnp.zeros(w.shape, jnp.float32) for w in weights))
    sums, (results, d_inputs) = lax.scan(one, start, (tokens, span_order, d_out))
    return (results, d_inputs, sums[0], sums[1], sums[2], sums[3], sums[4])
```

```python
import jax
import jax.numpy as jnp
import numpy as np
from jax import lax
from jax.sharding import Mesh
from jax.sharding import PartitionSpec as P

D = 1024
H = 16
KVH = 8
HD = 64
FF = 4608
LOC = 128
SPAN = 64
SPANS = 32
DP = ("z", "core")
SEQ = ("x", "y")
ALL = ("z", "core", "x", "y")
UNITS = FF // 8
PAD = 640

EPSILON = 1e-05
THETA = 1000000.0
BF = jnp.bfloat16
F32 = jnp.float32

UP = [(i, (i + 1) % 4) for i in range(4)]
DOWN = [(i, (i - 1) % 4) for i in range(4)]
SWAP = [(0, 1), (1, 0)]


def gather_dp(x):
    half = x.shape[0] // 2
    a = lax.ppermute(x, "z", UP)
    b = lax.ppermute(x, "z", DOWN)
    c0 = lax.ppermute(a[:half], "z", UP)
    c1 = lax.ppermute(b[half:], "z", DOWN)
    x_, a_, b_, c0_, c1_ = [lax.ppermute(v, "core", SWAP) for v in (x, a, b, c0, c1)]
    return [x, x_, a, a_, jnp.concatenate([c0, c1]), jnp.concatenate([c0_, c1_]), b, b_]


def scatter_dp(keep, give):
    half = keep.shape[1] // 2
    got = lax.ppermute(give, "core", SWAP)
    s = (keep.astype(F32) + got.astype(F32)).astype(BF)
    r0 = lax.ppermute(s[2, :half], "z", UP)
    r1 = lax.ppermute(s[2, half:], "z", DOWN)
    e3 = lax.ppermute(s[3, half:], "z", UP)
    e1 = lax.ppermute(s[1, :half], "z", DOWN)
    f3 = lax.ppermute((s[3, :half].astype(F32) + r0.astype(F32)).astype(BF), "z", UP)
    f1 = lax.ppermute((s[1, half:].astype(F32) + r1.astype(F32)).astype(BF), "z", DOWN)
    top = s[0, :half].astype(F32) + f3.astype(F32) + e1.astype(F32)
    low = s[0, half:].astype(F32) + e3.astype(F32) + f1.astype(F32)
    return jnp.concatenate([top, low])


def swap_all(x, axes):
    return lax.all_to_all(x, axes, split_axis=0, concat_axis=0, tiled=True)


def angles(positions):
    half = HD // 2
    freqs = THETA ** (-(jnp.arange(half, dtype=F32) * 2.0 / HD))
    turned = positions.astype(F32)[..., None] * freqs
    return jnp.cos(turned), jnp.sin(turned)


def rotate(values, cosine, sine):
    half = HD // 2
    a = values[..., :half]
    b = values[..., half:]
    return jnp.concatenate([a * cosine - b * sine, b * cosine + a * sine], axis=-1)


def unrotate(values, cosine, sine):
    return rotate(values, cosine, -sine)


def inv_rms(x):
    return lax.rsqrt(jnp.mean(x * x, axis=-1, keepdims=True) + EPSILON)


def rms_back(d_gained, unit, inv_scale, gain):
    d_unit = d_gained * gain
    return inv_scale * (d_unit - unit * jnp.mean(d_unit * unit, axis=-1, keepdims=True))


def dot(spec, a, b):
    return jnp.einsum(spec, a, b, preferred_element_type=F32)


def to_slots(x):
    return x.reshape(16, 2, 64, 64).transpose(0, 2, 1, 3).reshape(16, 64, 128)


def from_slots(x):
    return x.reshape(16, 64, 2, 64).transpose(0, 2, 1, 3).reshape(2048, 64)


def on_device(tokens, w_qkv, w_out, w_gu, w_down, gains, span_order, d_out):
    z = lax.axis_index("z")
    core = lax.axis_index("core")
    s = lax.axis_index(SEQ)
    rel = np.arange(8)
    b_of = 2 * ((z - rel // 2) % 4) + (core ^ (rel % 2))
    ab = np.arange(8)
    r_of = 2 * ((z - ab // 2) % 4) + (core ^ (ab % 2))

    wq = w_qkv[:, :1024].reshape(8, 8, 128)
    wkv = jnp.concatenate(
        [w_qkv[:, 1024:1536].reshape(8, 8, 64), w_qkv[:, 1536:].reshape(8, 8, 64)], axis=-1
    )
    extra = jnp.concatenate([gains, span_order[0].astype(BF), jnp.zeros((79,), BF)])
    pay = jnp.concatenate(
        [wq.transpose(1, 0, 2), wkv.transpose(1, 0, 2), jnp.broadcast_to(extra, (8, 8, 128))], axis=1
    )
    pay = jnp.broadcast_to(pay[:, None], (8, 16, 24, 128)).reshape(128, 24, 128)
    got = swap_all(pay, ALL)
    w_j = jnp.concatenate(
        [got[:, :8].reshape(1024, 128), got[:, 8:16].reshape(1024, 128)], axis=1
    )
    gain_all = got[:, 16, :17].reshape(2176).astype(F32)
    orders = got.reshape(8, 16, 24, 128)[:, 0, 16, 17:49].astype(jnp.int32)
    a_gain = gain_all[:1024]
    f_gain = gain_all[1024:2048]
    q_gain = gain_all[2048:2112]
    k_gain = gain_all[2112:]

    x_all = jnp.concatenate(gather_dp(tokens[0])).astype(F32)

    def cut(w):
        return jnp.pad(w.reshape(8, 8, UNITS), ((0, 0), (0, 0), (0, PAD - UNITS))).transpose(1, 0, 2)

    ff_pay = jnp.concatenate([cut(w_gu[:, :FF]), cut(w_gu[:, FF:]), cut(w_down)], axis=-1)
    ff_got = swap_all(ff_pay, DP)
    seq_pay = jnp.concatenate([ff_got, w_out.reshape(8, 8, 128).transpose(1, 0, 2)], axis=-1)
    seq_got = lax.all_gather(seq_pay, SEQ, axis=1, tiled=False)
    w_gu_j = seq_got[..., : 2 * PAD].reshape(1024, 2 * PAD)
    w_down_j = seq_got[..., 2 * PAD : 3 * PAD].reshape(1024, PAD)
    w_out_j = seq_got[..., 3 * PAD :].transpose(1, 2, 0, 3).reshape(128, 1024)
    w_out_rel = jnp.concatenate(gather_dp(w_out_j))
    d_all = jnp.concatenate(gather_dp(d_out[0]))

    r1 = inv_rms(x_all)
    n1 = x_all * r1
    h = (n1 * a_gain).astype(BF)
    mixed = dot("rd,df->rf", h, w_j)
    q_raw = mixed[:, :128].reshape(8, 128, 2, 64)
    k_raw = mixed[:, 128:192].reshape(8, 128, 1, 64)
    v_raw = mixed[:, 192:].reshape(8, 128, 64)
    own_orders = lax.dynamic_slice_in_dim(orders, 2 * s, 2, 1)[b_of]
    t = np.arange(128)
    cosine, sine = angles(own_orders[:, t // 64] * 64 + t % 64)
    cosine, sine = cosine[:, :, None], sine[:, :, None]
    rq = inv_rms(q_raw)
    qn = q_raw * rq
    q_rot = rotate(qn * q_gain, cosine, sine).astype(BF)
    rk = inv_rms(k_raw)
    kn = k_raw * rk
    k_rot = rotate(kn * k_gain, cosine, sine).astype(BF)

    kv = jnp.concatenate([k_rot[:, :, 0], v_raw.astype(BF)], axis=-1)
    q_send = q_rot.reshape(8, 2, 64, 2, 64).transpose(0, 3, 2, 1, 4).reshape(8, 2, 64, 128)
    send = jnp.concatenate([jnp.broadcast_to(kv[:, None], (8, 2, 128, 128)), q_send], axis=2)
    qkv = swap_all(send[r_of].reshape(16, 192, 128), SEQ)

    keys = qkv[:, :128, :64].reshape(2048, 64)
    values = qkv[:, :128, 64:].reshape(2048, 64)
    queries = from_slots(qkv[:, 128:])
    order = lax.dynamic_index_in_dim(orders, s // 2, 0, False)
    tt = np.arange(2048)
    pos = order[tt // 64] * 64 + tt % 64
    allowed = pos[:, None] >= pos[None, :]
    scale = HD**-0.5

    def scores_of():
        return jnp.where(allowed, dot("qd,td->qt", queries, keys) * scale, -1e30)

    scores = scores_of()
    top = jnp.max(scores, axis=-1, keepdims=True)
    weights = jnp.exp(scores - top)
    total = jnp.sum(weights, axis=-1, keepdims=True)
    probs = weights / total
    o = dot("qt,td->qd", probs.astype(BF), values)
    lse = top + jnp.log(total)
    o_bf = o.astype(BF)
    o_got = swap_all(to_slots(o_bf), SEQ)
    attn_j = o_got.reshape(8, 2, 64, 2, 64).transpose(0, 3, 2, 1, 4).reshape(1024, 128)
    attn = jnp.concatenate(gather_dp(attn_j), axis=1)
    attn = attn.reshape(8, 128, 1024)[b_of].reshape(1024, 1024)

    x1 = x_all + dot("rd,de->re", attn, w_out_rel)
    r2 = inv_rms(x1)
    n2 = x1 * r2
    h2 = (n2 * f_gain).astype(BF)
    gate_up = dot("rd,dc->rc", h2, w_gu_j)
    gate = gate_up[:, :PAD]
    upper = gate_up[:, PAD:]
    sigma = jax.nn.sigmoid(gate)
    swish = gate * sigma
    act = (swish * upper).astype(BF)
    d_act = dot("rd,dc->rc", d_all, w_down_j).astype(BF).astype(F32)
    d_gate = d_act * upper * (sigma * (1.0 + gate * (1.0 - sigma)))
    d_gu = jnp.concatenate([d_gate, d_act * swish], axis=1).astype(BF)
    d_h2_part = dot("rc,dc->rd", d_gu, w_gu_j)
    d_h2_four = d_h2_part.astype(BF).reshape(4, 2, 128, 1024)
    d_h2 = scatter_dp(d_h2_four[:, 0], d_h2_four[:, 1])
    gf_part = jnp.sum(d_h2_part * n2, axis=0)
    out_part = dot("rc,dc->rd", act, w_down_j).astype(BF).reshape(4, 2, 128, 1024)
    result = x1[:128] + scatter_dp(out_part[:, 0], out_part[:, 1])
    g_gu_j = dot("rd,rc->dc", h2, d_gu)
    g_down_j = dot("rd,rc->dc", d_all, act)
    g_ff = jnp.concatenate([g_gu_j, g_down_j], axis=1).astype(BF)
    g_ff = g_ff.reshape(8, 16, 8, 3 * PAD).transpose(1, 0, 2, 3)
    g_ff = jnp.sum(swap_all(g_ff.reshape(16, 64, 3 * PAD), SEQ).astype(F32), axis=0).astype(BF)
    g_ff = swap_all(g_ff.reshape(8, 8, 3 * PAD), DP).astype(F32)
    g_ff = g_ff.reshape(8, 8, 3, PAD)[..., :UNITS].transpose(2, 1, 0, 3).reshape(3, 8, FF)
    g_gu = jnp.concatenate([g_ff[0], g_ff[1]], axis=1)
    g_down = g_ff[2]

    d_x1 = d_out[0].astype(F32) + rms_back(d_h2, n2[:128], r2[:128], f_gain)
    d_branch = d_x1.astype(BF)
    d_attn = dot("re,de->rd", d_branch, w_out_rel).astype(BF).reshape(2, 64, 8, 2, 64)
    d_attn = d_attn.transpose(2, 3, 1, 0, 4)[r_of].reshape(8, 2, 64, 128)
    d_attn = swap_all(d_attn, DP)
    d_o = from_slots(swap_all(d_attn.reshape(16, 64, 128), SEQ))
    branch_all = jnp.concatenate(gather_dp(d_branch)).reshape(8, 128, 1024)[r_of].reshape(1024, 1024)
    g_out_j = dot("rd,re->de", attn_j, branch_all)
    g_out_send = g_out_j.astype(BF).reshape(16, 8, 8, 128).transpose(0, 2, 1, 3).reshape(16, 64, 128)

    probs = jnp.exp(scores_of() - lse)
    d_probs = dot("qd,td->qt", d_o, values)
    delta = jnp.sum(d_o.astype(F32) * o, axis=-1, keepdims=True)
    d_scores = (probs * (d_probs - delta)).astype(BF)
    d_q = dot("qt,td->qd", d_scores, keys) * scale
    d_k = dot("qt,qd->td", d_scores, queries) * scale
    d_v = dot("qt,qd->td", probs.astype(BF), d_o)
    d_kv = jnp.concatenate([d_k, d_v], axis=1).astype(BF).reshape(16, 128, 128)
    back = swap_all(jnp.concatenate([d_kv, to_slots(d_q.astype(BF)), g_out_send], axis=1), SEQ)
    g_out = jnp.sum(back[:, 192:].astype(F32), axis=0)
    g_out = g_out.reshape(8, 8, 128).transpose(1, 0, 2).reshape(8, 1024)

    back = back[:, :192].reshape(8, 2, 192, 128)[b_of].astype(F32)
    d_kv = jnp.sum(back[:, :, :128], axis=1)
    d_q = back[:, :, 128:].reshape(8, 2, 64, 2, 64).transpose(0, 3, 2, 1, 4).reshape(8, 128, 2, 64)
    dq_g = unrotate(d_q, cosine, sine)
    gq_part = jnp.sum(dq_g * qn, axis=(0, 1, 2))
    dq_raw = rms_back(dq_g, qn, rq, q_gain)
    dk_g = unrotate(d_kv[:, :, None, :64], cosine, sine)
    gk_part = jnp.sum(dk_g * kn, axis=(0, 1, 2))
    dk_raw = rms_back(dk_g, kn, rk, k_gain)
    d_mixed = jnp.concatenate(
        [dq_raw.reshape(1024, 128), dk_raw.reshape(1024, 64), d_kv[:, :, 64:].reshape(1024, 64)], axis=1
    ).astype(BF)
    d_h_part = dot("rf,df->rd", d_mixed, w_j)
    ga_part = jnp.sum(d_h_part * n1, axis=0)
    d_h_four = d_h_part.astype(BF).reshape(4, 2, 128, 1024)
    d_h = scatter_dp(d_h_four[:, 0], d_h_four[:, 1])
    d_tokens = d_x1 + rms_back(d_h, n1[:128], r1[:128], a_gain)

    g_qkv_j = dot("rd,rf->df", h, d_mixed).astype(BF).reshape(128, 8, 256)
    g_gain = jnp.concatenate([ga_part, gf_part, gq_part, gk_part]).reshape(128, 17)
    gain_hi = g_gain.astype(BF)
    gain_lo = (g_gain - gain_hi.astype(F32)).astype(BF)
    gain_rows = jnp.concatenate([gain_hi, gain_lo, jnp.zeros((128, 94), BF)], axis=1)
    gain_rows = jnp.broadcast_to(gain_rows[:, None], (128, 8, 128))
    last = swap_all(
        jnp.concatenate([g_qkv_j[:, :, :128], g_qkv_j[:, :, 128:], gain_rows], axis=1), ALL
    ).astype(F32)
    g_gains = jnp.sum(last[:, 16, :17] + last[:, 16, 17:34], axis=0)
    last = jnp.sum(last.reshape(8, 16, 24, 128), axis=1)
    g_qkv = jnp.concatenate(
        [
            last[:, :8].transpose(1, 0, 2).reshape(8, 1024),
            last[:, 8:16, :64].transpose(1, 0, 2).reshape(8, 512),
            last[:, 8:16, 64:].transpose(1, 0, 2).reshape(8, 512),
        ],
        axis=1,
    )
    return (
        result.astype(BF)[None],
        d_tokens[None],
        g_qkv,
        g_out,
        g_gu,
        g_down,
        g_gains,
    )


def solution(mesh):
    split = Mesh(mesh.devices.reshape(4, 2, 4, 4), ALL)
    return jax.shard_map(
        on_device,
        mesh=split,
        in_specs=(
            P(DP, SEQ, None),
            P(ALL, None),
            P(ALL, None),
            P(ALL, None),
            P(ALL, None),
            P(ALL),
            P(DP, None),
            P(DP, SEQ, None),
        ),
        out_specs=(
            P(DP, SEQ, None),
            P(DP, SEQ, None),
            P(ALL, None),
            P(ALL, None),
            P(ALL, None),
            P(ALL, None),
            P(ALL),
        ),
        check_vma=False,
    )
```

```python
import jax
import jax.numpy as jnp
import numpy as np
from jax import lax
from jax.experimental import pallas as pl
from jax.experimental.pallas import tpu as pltpu
from jax.sharding import Mesh
from jax.sharding import PartitionSpec as P

D = 1024
H = 16
KVH = 8
HD = 64
FF = 4608
LOC = 128
SPAN = 64
SPANS = 32
DP = ("z", "core")
SEQ = ("x", "y")
ALL = ("z", "core", "x", "y")
UNITS = FF // 8
PAD = 640

EPSILON = 1e-05
THETA = 1000000.0
BF = jnp.bfloat16
F32 = jnp.float32

UP = [(i, (i + 1) % 4) for i in range(4)]
DOWN = [(i, (i - 1) % 4) for i in range(4)]
SWAP = [(0, 1), (1, 0)]


def params(mb):
    return pltpu.CompilerParams(vmem_limit_bytes=mb * 2**20)


def shape(dims, kind=BF):
    return jax.ShapeDtypeStruct(dims, kind)


SMEM = pl.BlockSpec(memory_space=pltpu.SMEM)
VMEM = pl.BlockSpec(memory_space=pltpu.VMEM)


def lane_tables():
    freqs = THETA ** (-(np.arange(HD // 2) * 2.0 / HD))
    lanes = freqs[np.arange(128) % (HD // 2)]
    far = (np.arange(SPANS) * SPAN)[:, None] * lanes[None]
    near = np.arange(SPAN)[:, None] * lanes[None]
    return [f(a).astype(np.float32) for a in (far, near) for f in (np.cos, np.sin)]


def gather_dp(x):
    half = x.shape[0] // 2
    a = lax.ppermute(x, "z", UP)
    b = lax.ppermute(x, "z", DOWN)
    c0 = lax.ppermute(a[:half], "z", UP)
    c1 = lax.ppermute(b[half:], "z", DOWN)
    x_, a_, b_, c0_, c1_ = [lax.ppermute(v, "core", SWAP) for v in (x, a, b, c0, c1)]
    return [x, x_, a, a_, c0, c1, c0_, c1_, b, b_]


def piece(refs, r):
    if r < 4:
        return refs[r][...]
    if r < 6:
        return jnp.concatenate([refs[4 + 2 * (r - 4)][...], refs[5 + 2 * (r - 4)][...]], axis=0)
    return refs[r + 2][...]


def sequence_of(r):
    z = lax.axis_index("z")
    core = lax.axis_index("core")
    other = core if r % 2 == 0 else 1 - core
    return 2 * lax.rem(z + 4 - r // 2, 4) + other


def scatter_dp(keep, give):
    half = keep.shape[1] // 2
    got = lax.ppermute(give, "core", SWAP)
    s = [(keep[o].astype(F32) + got[o].astype(F32)).astype(BF) for o in range(4)]
    r0 = lax.ppermute(s[2][:half], "z", UP)
    r1 = lax.ppermute(s[2][half:], "z", DOWN)
    e3 = lax.ppermute(s[3][half:], "z", UP)
    e1 = lax.ppermute(s[1][:half], "z", DOWN)
    f3 = lax.ppermute((s[3][:half].astype(F32) + r0.astype(F32)).astype(BF), "z", UP)
    f1 = lax.ppermute((s[1][half:].astype(F32) + r1.astype(F32)).astype(BF), "z", DOWN)
    top = s[0][:half].astype(F32) + f3.astype(F32) + e1.astype(F32)
    low = s[0][half:].astype(F32) + e3.astype(F32) + f1.astype(F32)
    return jnp.concatenate([top, low])


def swap_all(x, axes):
    return lax.all_to_all(x, axes, split_axis=0, concat_axis=0, tiled=True)


def rms_back(d_gained, unit, inv_scale, gain):
    d_unit = d_gained * gain
    return inv_scale * (d_unit - unit * jnp.mean(d_unit * unit, axis=-1, keepdims=True))


def inv_rms(x):
    return lax.rsqrt(jnp.mean(x * x, axis=-1, keepdims=True) + EPSILON)


def dot(spec, a, b):
    return jnp.einsum(spec, a, b, preferred_element_type=F32)


def mm(a, b, ca=1, cb=0):
    return lax.dot_general(a, b, (((ca,), (cb,)), ((), ())), preferred_element_type=F32)


def lanes_of(rows):
    return lax.broadcasted_iota(jnp.int32, (rows, 128), 1)


def head_mean(v, lane):
    low = jnp.sum(jnp.where(lane < 64, v, 0.0), axis=-1, keepdims=True)
    high = jnp.sum(jnp.where(lane < 64, 0.0, v), axis=-1, keepdims=True)
    return jnp.where(lane < 64, low, high) * (1.0 / HD)


def partner(v, lane):
    return jnp.where((lane & 32) == 0, pltpu.roll(v, 96, 1), pltpu.roll(v, 32, 1))


def trig(tables, orders_ref, b):
    cf, sf, cn, sn = tables
    s = lax.axis_index(SEQ)
    sign = jnp.where((lanes_of(SPAN) & 32) == 0, -1.0, 1.0)
    cos, sin = [], []
    for k in range(2):
        span = orders_ref[b, 2 * s + k]
        c, d = cf[pl.ds(span, 1), :], sf[pl.ds(span, 1), :]
        cos.append(c * cn[...] - d * sn[...])
        sin.append((d * cn[...] + c * sn[...]) * sign)
    return jnp.concatenate(cos), jnp.concatenate(sin)


def project_kernel(*refs):
    toks = refs[:10]
    got_ref, a_gain, qk_gain, orders_ref = refs[10:14]
    tables = refs[14:18]
    send_ref, h_ref, mixed_ref, w_ref, wout_ref, w32, wout32 = refs[18:]
    for s in range(16):
        block = got_ref[s, 0:192, :].astype(F32)
        for j in range(8):
            at = 128 * j + 8 * s
            w32[at : at + 8, :128] = block[8 * j : 8 * j + 8]
            w32[at : at + 8, 128:] = block[64 + 8 * j : 72 + 8 * j]
            wout32[8 * s : 8 * s + 8, 128 * j : 128 * j + 128] = block[128 + 8 * j : 136 + 8 * j]
    w_ref[...] = w32[...].astype(BF)
    wout_ref[...] = wout32[...].astype(BF)
    lane = lanes_of(128)
    low = lane < 64
    for r in range(8):
        x = piece(toks, r).astype(F32)
        h = (x * inv_rms(x) * a_gain[...]).astype(BF)
        h_ref[128 * r : 128 * r + 128, :] = h
        mixed = mm(h, w_ref[...])
        mixed_ref[128 * r : 128 * r + 128, :] = mixed
        b = sequence_of(r)
        cos, sin = trig(tables, orders_ref, b)

        def turned(v, gain):
            g = v * lax.rsqrt(head_mean(v * v, lane) + EPSILON) * gain
            return g * cos + partner(g, lane) * sin

        q = turned(mixed[:, :128], qk_gain[0:1, :])
        kv = jnp.where(low, turned(mixed[:, 128:], qk_gain[1:2, :]), mixed[:, 128:]).astype(BF)
        flip = pltpu.roll(q, 64, 1)
        l64 = low[:64]
        send_ref[2 * b, 0:128, :] = kv
        send_ref[2 * b + 1, 0:128, :] = kv
        send_ref[2 * b, 128:192, :] = jnp.where(l64, q[:64], flip[64:]).astype(BF)
        send_ref[2 * b + 1, 128:192, :] = jnp.where(l64, flip[:64], q[64:]).astype(BF)


def project(toks, got, a_gain, qk_gain, orders, tables):
    return pl.pallas_call(
        project_kernel,
        out_shape=[
            shape((16, 192, 128)),
            shape((1024, 1024)),
            shape((1024, 256), F32),
            shape((1024, 256)),
            shape((128, 1024)),
        ],
        in_specs=[VMEM] * 13 + [SMEM] + [VMEM] * 4,
        out_specs=[VMEM] * 5,
        scratch_shapes=[pltpu.VMEM((1024, 256), F32), pltpu.VMEM((128, 1024), F32)],
        compiler_params=params(40),
        cost_estimate=pl.CostEstimate(flops=2 * 1024 * 1024 * 256, bytes_accessed=8 << 20, transcendentals=0),
    )(*toks, got, a_gain, qk_gain, orders, *tables)


def attend_kernel(qkv_ref, orders_ref, send_ref, q_ref, kv_ref, ot_ref, lse_ref, kvt, osc):
    b = lax.axis_index(SEQ) // 2
    l64 = lanes_of(64) < 64
    for i in range(32):
        at = pl.multiple_of(orders_ref[b, i] * 64, 64)
        kv_ref[pl.ds(at, 64), :] = qkv_ref[i // 2, 64 * (i % 2) : 64 * (i % 2) + 64, :]
        block = qkv_ref[i // 2, 128:192, :].astype(F32)
        if i % 2:
            block = pltpu.roll(block, 64, 1)
        q_ref[pl.ds(at, 64), :] = jnp.where(l64, block * HD**-0.5, 0.0).astype(BF)
    kvt[...] = kv_ref[...].T
    after = lax.broadcasted_iota(jnp.int32, (256, 256), 0) > lax.broadcasted_iota(
        jnp.int32, (256, 256), 1
    )
    for i in range(8):
        n = 256 * i
        q = q_ref[n : n + 256, :]
        near = jnp.where(after, -1e30, mm(kv_ref[n : n + 256, :], q, 1, 1))
        top = jnp.max(near, axis=0, keepdims=True)
        if i:
            far = mm(kv_ref[:n, :], q, 1, 1)
            top = jnp.maximum(top, jnp.max(far, axis=0, keepdims=True))
        near = jnp.exp(near - top)
        total = jnp.sum(near, axis=0, keepdims=True)
        o = mm(kvt[:, n : n + 256], near.astype(BF))
        if i:
            far = jnp.exp(far - top)
            total = total + jnp.sum(far, axis=0, keepdims=True)
            o = o + mm(kvt[:, :n], far.astype(BF))
        o = o / total
        ot_ref[:, n : n + 256] = o[64:]
        lse_ref[:, n : n + 256] = top + jnp.log(total)
        osc[n : n + 256, :] = o.T
    for i in range(16):
        a = osc[pl.ds(pl.multiple_of(orders_ref[b, 2 * i] * 64, 64), 64), :]
        c = osc[pl.ds(pl.multiple_of(orders_ref[b, 2 * i + 1] * 64, 64), 64), :]
        send_ref[i] = jnp.where(l64, pltpu.roll(a, 64, 1), c).astype(BF)


def attend(qkv, orders):
    return pl.pallas_call(
        attend_kernel,
        out_shape=[
            shape((16, 64, 128)),
            shape((2048, 128)),
            shape((2048, 128)),
            shape((64, 2048), F32),
            shape((1, 2048), F32),
        ],
        in_specs=[VMEM, SMEM],
        out_specs=[VMEM] * 5,
        scratch_shapes=[pltpu.VMEM((128, 2048), BF), pltpu.VMEM((2048, 128), F32)],
        compiler_params=params(40),
        cost_estimate=pl.CostEstimate(flops=2 * 2048 * 2048 * 128, bytes_accessed=4 << 20, transcendentals=2 << 20),
    )(qkv, orders)


def attend_back_kernel(
    got_ref, q_ref, kv_ref, ot_ref, lse_ref, orders_ref, send_ref, do, kvt, dkv, dqs
):
    b = lax.axis_index(SEQ) // 2
    l64 = lanes_of(64) < 64
    for i in range(32):
        at = pl.multiple_of(orders_ref[b, i] * 64, 64)
        block = got_ref[i // 2].astype(F32)
        if i % 2 == 0:
            block = pltpu.roll(block, 64, 1)
        do[pl.ds(at, 64), :] = jnp.where(l64, 0.0, block)
    kvt[...] = kv_ref[...].T
    before = lax.broadcasted_iota(jnp.int32, (256, 256), 0) <= lax.broadcasted_iota(
        jnp.int32, (256, 256), 1
    )
    dkv[...] = jnp.zeros_like(dkv)
    for i in range(8):
        n = 256 * i
        q = q_ref[n : n + 256, :]
        d32 = do[n : n + 256, :]
        d = d32.astype(BF)
        lse = lse_ref[:, n : n + 256]
        delta = jnp.sum(ot_ref[:, n : n + 256] * d32.T[64:], axis=0, keepdims=True)
        dq = None
        for lo, hi in ((n, n + 256), (0, n)):
            if lo == hi:
                continue
            keys = kv_ref[lo:hi, :]
            p = jnp.exp(mm(keys, q, 1, 1) - lse)
            if lo:
                p = jnp.where(before, p, 0.0)
            elif hi == 256 and n == 0:
                p = jnp.where(before, p, 0.0)
            ds = (p * (mm(keys, d, 1, 1) - delta)).astype(BF)
            dkv[lo:hi, :] += mm(ds, q) + mm(p.astype(BF), d)
            term = mm(kvt[:, lo:hi], ds)
            dq = term if dq is None else dq + term
        dqs[n : n + 256, :] = (dq * HD**-0.5).T
    for i in range(16):
        at = pl.multiple_of(orders_ref[b, 2 * i] * 64, 64)
        bt = pl.multiple_of(orders_ref[b, 2 * i + 1] * 64, 64)
        send_ref[i, 0:64, :] = dkv[pl.ds(at, 64), :].astype(BF)
        send_ref[i, 64:128, :] = dkv[pl.ds(bt, 64), :].astype(BF)
        send_ref[i, 128:192, :] = jnp.where(
            l64, dqs[pl.ds(at, 64), :], pltpu.roll(dqs[pl.ds(bt, 64), :], 64, 1)
        ).astype(BF)


def attend_back(got, q, kv, ot, lse, orders):
    return pl.pallas_call(
        attend_back_kernel,
        out_shape=shape((16, 192, 128)),
        in_specs=[VMEM] * 5 + [SMEM],
        out_specs=VMEM,
        scratch_shapes=[
            pltpu.VMEM((2048, 128), F32),
            pltpu.VMEM((128, 2048), BF),
            pltpu.VMEM((2048, 128), F32),
            pltpu.VMEM((2048, 128), F32),
        ],
        compiler_params=params(40),
        cost_estimate=pl.CostEstimate(flops=5 * 2048 * 2048 * 128, bytes_accessed=4 << 20, transcendentals=2 << 20),
    )(got, q, kv, ot, lse, orders)


def feed_kernel(*refs):
    toks, douts, attns, wouts = refs[:10], refs[10:20], refs[20:30], refs[30:40]
    f_gain, w_ref = refs[40:42]
    keep_ref, give_ref, x1_ref, h2_ref, act_ref, dgu_ref, gf_ref, wo, atn = refs[42:]
    for r in range(8):
        wo[128 * r : 128 * r + 128, :] = piece(wouts, r)
        atn[r] = piece(attns, r)
    l64 = lanes_of(64) < 64
    gf = jnp.zeros((1, 1024), F32)
    for o in range(4):
        cols = []
        for k in range(8):
            rows = []
            for f in range(2):
                b = sequence_of(2 * o + f)
                a = atn[k, 2 * b].astype(F32)
                c = atn[k, 2 * b + 1].astype(F32)
                rows.append(jnp.where(l64, a, pltpu.roll(c, 64, 1)))
                rows.append(jnp.where(l64, pltpu.roll(a, 64, 1), c))
            cols.append(jnp.concatenate(rows).astype(BF))
        attn = jnp.concatenate(cols, axis=1)
        x = jnp.concatenate([piece(toks, 2 * o), piece(toks, 2 * o + 1)]).astype(F32)
        x1 = x + mm(attn, wo[...])
        if o == 0:
            x1_ref[...] = x1[:128]
        n2 = x1 * inv_rms(x1)
        h2 = (n2 * f_gain[...]).astype(BF)
        at = slice(256 * o, 256 * o + 256)
        h2_ref[at, :] = h2
        gate_up = mm(h2, w_ref[:, : 2 * PAD])
        gate, upper = gate_up[:, :PAD], gate_up[:, PAD:]
        sigma = jax.nn.sigmoid(gate)
        swish = gate * sigma
        act_ref[at, :] = (swish * upper).astype(BF)
        d = jnp.concatenate([piece(douts, 2 * o), piece(douts, 2 * o + 1)])
        d_act = mm(d, w_ref[:, 2 * PAD :]).astype(BF).astype(F32)
        d_gate = d_act * upper * (sigma * (1.0 + gate * (1.0 - sigma)))
        dgu_ref[at, :PAD] = d_gate.astype(BF)
        dgu_ref[at, PAD:] = (d_act * swish).astype(BF)
        d_h2 = mm(dgu_ref[at, :], w_ref[:, : 2 * PAD], 1, 1)
        gf = gf + jnp.sum(d_h2 * n2, axis=0, keepdims=True)
        keep_ref[o] = d_h2[:128].astype(BF)
        give_ref[o] = d_h2[128:].astype(BF)
    gf_ref[...] = gf


def feed(toks, douts, attns, wouts, f_gain, w_ff):
    return pl.pallas_call(
        feed_kernel,
        out_shape=[
            shape((4, 128, 1024)),
            shape((4, 128, 1024)),
            shape((128, 1024), F32),
            shape((1024, 1024)),
            shape((1024, PAD)),
            shape((1024, 2 * PAD)),
            shape((1, 1024), F32),
            shape((1024, 1024)),
        ],
        in_specs=[VMEM] * 42,
        out_specs=[VMEM] * 8,
        scratch_shapes=[pltpu.VMEM((8, 16, 64, 128), BF)],
        compiler_params=params(56),
        cost_estimate=pl.CostEstimate(flops=2 * 1024 * 1024 * 4224, bytes_accessed=24 << 20, transcendentals=1 << 20),
    )(*toks, *douts, *attns, *wouts, f_gain, w_ff)


def unproject_kernel(*refs):
    toks = refs[:10]
    back_ref, mixed_ref, w_ref, qk_gain, orders_ref = refs[10:15]
    tables = refs[15:19]
    keep_ref, give_ref, dm_ref, ga_ref, gqk_ref = refs[19:]
    lane = lanes_of(128)
    low = lane < 64
    ga = jnp.zeros((1, 1024), F32)
    gq = jnp.zeros((1, 128), F32)
    gk = jnp.zeros((1, 128), F32)
    for r in range(8):
        b = sequence_of(r)
        cos, sin = trig(tables, orders_ref, b)
        mixed = mixed_ref[128 * r : 128 * r + 128, :]
        u = back_ref[2 * b, 0:192, :].astype(F32)
        v = back_ref[2 * b + 1, 0:192, :].astype(F32)
        d_kv = u[:128] + v[:128]
        u, v = u[128:], v[128:]
        l64 = low[:64]
        d_q = jnp.concatenate(
            [
                jnp.where(l64, u, pltpu.roll(v, 64, 1)),
                jnp.where(l64, pltpu.roll(u, 64, 1), v),
            ]
        )

        def turned_back(d, raw, gain):
            scale = lax.rsqrt(head_mean(raw * raw, lane) + EPSILON)
            unit = raw * scale
            g = d * cos - partner(d, lane) * sin
            e = g * gain
            grad = jnp.sum(g * unit, axis=0, keepdims=True)
            return scale * (e - unit * head_mean(e * unit, lane)), grad

        dq_raw, grad_q = turned_back(d_q, mixed[:, :128], qk_gain[0:1, :])
        dk_raw, grad_k = turned_back(d_kv, mixed[:, 128:], qk_gain[1:2, :])
        gq, gk = gq + grad_q, gk + grad_k
        at = slice(128 * r, 128 * r + 128)
        dm_ref[at, :128] = dq_raw.astype(BF)
        dm_ref[at, 128:] = jnp.where(low, dk_raw, d_kv).astype(BF)
        d_h = mm(dm_ref[at, :], w_ref[...], 1, 1)
        x = piece(toks, r).astype(F32)
        ga = ga + jnp.sum(d_h * (x * inv_rms(x)), axis=0, keepdims=True)
        (give_ref if r % 2 else keep_ref)[r // 2] = d_h.astype(BF)
    ga_ref[...] = ga
    gqk_ref[0:1, :] = gq
    gqk_ref[1:2, :] = gk


def unproject(toks, back, mixed, w, qk_gain, orders, tables):
    return pl.pallas_call(
        unproject_kernel,
        out_shape=[
            shape((4, 128, 1024)),
            shape((4, 128, 1024)),
            shape((1024, 256)),
            shape((1, 1024), F32),
            shape((2, 128), F32),
        ],
        in_specs=[VMEM] * 14 + [SMEM] + [VMEM] * 4,
        out_specs=[VMEM] * 5,
        compiler_params=params(40),
        cost_estimate=pl.CostEstimate(flops=2 * 1024 * 1024 * 256, bytes_accessed=8 << 20, transcendentals=0),
    )(*toks, back, mixed, w, qk_gain, orders, *tables)


def on_device(tokens, w_qkv, w_out, w_gu, w_down, gains, span_order, d_out):
    z = lax.axis_index("z")
    core = lax.axis_index("core")
    ab = np.arange(8)
    r_of = 2 * ((z - ab // 2) % 4) + (core ^ (ab % 2))
    tables = [jnp.asarray(a) for a in lane_tables()]

    def cut(w):
        return jnp.pad(w.reshape(8, 8, UNITS), ((0, 0), (0, 0), (0, PAD - UNITS)))

    extra = jnp.concatenate([gains, span_order[0].astype(BF), jnp.zeros((79,), BF)])
    pay = jnp.concatenate(
        [
            cut(w_gu[:, :FF]),
            cut(w_gu[:, FF:]),
            cut(w_down),
            w_qkv[:, :1024].reshape(8, 8, 128),
            w_qkv[:, 1024:1536].reshape(8, 8, 64),
            w_qkv[:, 1536:].reshape(8, 8, 64),
            jnp.broadcast_to(extra, (8, 8, 128)),
        ],
        axis=-1,
    ).transpose(1, 0, 2)
    dp_got = swap_all(pay, DP)
    toks = gather_dp(tokens[0])
    seq_pay = jnp.concatenate(
        [
            dp_got[:, :, 1920:2048].reshape(64, 128),
            dp_got[:, :, 2048:2176].reshape(64, 128),
            w_out.reshape(8, 8, 128).transpose(1, 0, 2).reshape(64, 128),
            dp_got[:, 0, 2176:],
            jnp.zeros((8, 128), BF),
        ]
    )
    got = swap_all(jnp.broadcast_to(seq_pay, (16, 208, 128)), SEQ)
    w_ff = lax.all_gather(dp_got[:, :, :1920], SEQ, axis=1, tiled=False).reshape(1024, 1920)
    gain_all = got[:, 192:200, :17].transpose(1, 0, 2).reshape(2176).astype(F32)
    orders = got[0, 192:200, 17:49].astype(jnp.int32)
    a_gain = gain_all[None, :1024]
    f_gain = gain_all[None, 1024:2048]
    q_gain, k_gain = gain_all[2048:2112], gain_all[2112:]
    qk_gain = jnp.stack([jnp.concatenate([q_gain, q_gain]), jnp.concatenate([k_gain, k_gain])])

    send, h, mixed, w_j, w_out_j = project(toks, got, a_gain, qk_gain, orders, tables)
    qkv = swap_all(send, SEQ)
    wouts = gather_dp(w_out_j)
    douts = gather_dp(d_out[0])
    o_send, q_s, kv_s, ot, lse = attend(qkv, orders)
    o_got = swap_all(o_send, SEQ)
    attns = gather_dp(o_got)
    d_keep, d_give, x1, h2, act, d_gu, gf_part, w_out_rel = feed(
        toks, douts, attns, wouts, f_gain, w_ff
    )
    d_h2 = scatter_dp(d_keep, d_give)

    r2 = inv_rms(x1)
    n2 = x1 * r2
    d_x1 = d_out[0].astype(F32) + rms_back(d_h2, n2, r2, f_gain)
    d_branch = d_x1.astype(BF)
    d_attn = dot("re,de->rd", d_branch, w_out_rel).astype(BF).reshape(2, 64, 8, 2, 64)
    d_attn = d_attn.transpose(2, 3, 1, 0, 4)[r_of].reshape(8, 2, 64, 128)
    d_o = swap_all(swap_all(d_attn, DP).reshape(16, 64, 128), SEQ)

    w_down_j = w_ff[:, 2 * PAD :]
    out_part = dot("rc,dc->rd", act, w_down_j).astype(BF).reshape(4, 2, 128, 1024)
    result = x1 + scatter_dp(out_part[:, 0], out_part[:, 1])
    d_all = jnp.concatenate(
        [*douts[:4], douts[4], douts[5], douts[6], douts[7], douts[8], douts[9]]
    )
    g_gu_j = dot("rd,rc->dc", h2, d_gu).astype(BF)
    g_down_j = dot("rd,rc->dc", d_all, act).astype(BF)
    g_ff = jnp.concatenate([g_gu_j, g_down_j], axis=1)
    g_ff = g_ff.reshape(8, 16, 8, 3 * PAD).transpose(1, 0, 2, 3).reshape(16 * 64, 3 * PAD)
    g_ff = lax.psum_scatter(g_ff, SEQ, scatter_dimension=0, tiled=True)
    g_ff = swap_all(g_ff.reshape(8, 8, 3 * PAD), DP).astype(F32)
    g_ff = g_ff.reshape(8, 8, 3, PAD)[..., :UNITS].transpose(2, 1, 0, 3).reshape(3, 8, FF)
    g_gu = jnp.concatenate([g_ff[0], g_ff[1]], axis=1)
    g_down = g_ff[2]

    attn_j = o_got.reshape(8, 2, 64, 2, 64).transpose(0, 3, 2, 1, 4).reshape(1024, 128)
    branches = gather_dp(d_branch)
    branch_all = jnp.concatenate(branches).reshape(8, 128, 1024)[r_of].reshape(1024, 1024)
    g_out_j = dot("rd,re->de", attn_j, branch_all)
    g_out_send = g_out_j.astype(BF).reshape(16, 8, 8, 128).transpose(0, 2, 1, 3).reshape(16, 64, 128)
    d_send = attend_back(d_o, q_s, kv_s, ot, lse, orders)
    back = swap_all(jnp.concatenate([d_send, g_out_send], axis=1), SEQ)
    g_out = jnp.sum(back[:, 192:].astype(F32), axis=0)
    g_out = g_out.reshape(8, 8, 128).transpose(1, 0, 2).reshape(8, 1024)
    h_keep, h_give, d_mixed, ga_part, gqk_part = unproject(
        toks, back, mixed, w_j, qk_gain, orders, tables
    )
    d_h = scatter_dp(h_keep, h_give)
    x = tokens[0].astype(F32)
    r1 = inv_rms(x)
    d_tokens = d_x1 + rms_back(d_h, x * r1, r1, a_gain)

    g_qkv_j = dot("rd,rf->df", h, d_mixed).astype(BF).reshape(128, 8, 256)
    gq_part = gqk_part[0, :64] + gqk_part[0, 64:]
    g_gain = jnp.concatenate([ga_part[0], gf_part[0], gq_part, gqk_part[1, :64]]).reshape(128, 17)
    gain_hi = g_gain.astype(BF)
    gain_lo = (g_gain - gain_hi.astype(F32)).astype(BF)
    gain_rows = jnp.concatenate([gain_hi, gain_lo, jnp.zeros((128, 94), BF)], axis=1)
    gain_rows = jnp.broadcast_to(gain_rows[:, None], (128, 8, 128))
    last = swap_all(
        jnp.concatenate([g_qkv_j[:, :, :128], g_qkv_j[:, :, 128:], gain_rows], axis=1), ALL
    ).astype(F32)
    g_gains = jnp.sum(last[:, 16, :17] + last[:, 16, 17:34], axis=0)
    last = jnp.sum(last.reshape(8, 16, 24, 128), axis=1)
    g_qkv = jnp.concatenate(
        [
            last[:, :8].transpose(1, 0, 2).reshape(8, 1024),
            last[:, 8:16, :64].transpose(1, 0, 2).reshape(8, 512),
            last[:, 8:16, 64:].transpose(1, 0, 2).reshape(8, 512),
        ],
        axis=1,
    )
    return (
        result.astype(BF)[None],
        d_tokens[None],
        g_qkv,
        g_out,
        g_gu,
        g_down,
        g_gains,
    )


def solution(mesh):
    split = Mesh(mesh.devices.reshape(4, 2, 4, 4), ALL)
    return jax.shard_map(
        on_device,
        mesh=split,
        in_specs=(
            P(DP, SEQ, None),
            P(ALL, None),
            P(ALL, None),
            P(ALL, None),
            P(ALL, None),
            P(ALL),
            P(DP, None),
            P(DP, SEQ, None),
        ),
        out_specs=(
            P(DP, SEQ, None),
            P(DP, SEQ, None),
            P(ALL, None),
            P(ALL, None),
            P(ALL, None),
            P(ALL, None),
            P(ALL),
        ),
        check_vma=False,
    )
```

```python
import jax
import jax.numpy as jnp
import numpy as np
from jax import lax
from jax.experimental import pallas as pl
from jax.experimental.pallas import tpu as pltpu
from jax.sharding import Mesh
from jax.sharding import PartitionSpec as P

D = 1024
H = 16
KVH = 8
HD = 64
FF = 4608
LOC = 128
SPAN = 64
SPANS = 32
DP = ("z", "core")
SEQ = ("x", "y")
ALL = ("z", "core", "x", "y")
UNITS = FF // 8
PAD = 640

EPSILON = 1e-05
THETA = 1000000.0
BF = jnp.bfloat16
F32 = jnp.float32

UP = [(i, (i + 1) % 4) for i in range(4)]
DOWN = [(i, (i - 1) % 4) for i in range(4)]
ACROSS = [(i, (i + 2) % 4) for i in range(4)]
SWAP = [(0, 1), (1, 0)]


def params(mb):
    return pltpu.CompilerParams(vmem_limit_bytes=mb * 2**20)


def shape(dims, kind=BF):
    return pltpu.HBM(dims, kind)


SMEM = pl.BlockSpec(memory_space=pltpu.SMEM)
VMEM = pl.BlockSpec(memory_space=pltpu.VMEM)
ANY = pl.BlockSpec(memory_space=pl.ANY)


def whole(*dims):
    return pl.BlockSpec(dims, lambda i: (0,) * len(dims))


def rows(n, width):
    return pl.BlockSpec((n, width), lambda i: (i, 0))


def slow(x):
    return pl.CostEstimate(flops=x, bytes_accessed=0, transcendentals=0)


def far(x):
    return pltpu.with_memory_space_constraint(x, pltpu.HBM)


def lane_tables():
    freqs = THETA ** (-(np.arange(HD // 2) * 2.0 / HD))
    lanes = freqs[np.arange(128) % (HD // 2)]
    far = (np.arange(SPANS) * SPAN)[:, None] * lanes[None]
    near = np.arange(SPAN)[:, None] * lanes[None]
    return [f(a).astype(np.float32) for a in (far, near) for f in (np.cos, np.sin)]


def gather_dp(x):
    a = lax.ppermute(x, "z", UP)
    b = lax.ppermute(x, "z", DOWN)
    c = lax.ppermute(x, "z", ACROSS)
    pieces = []
    for v in (x, a, c, b):
        pieces += [v, lax.ppermute(v, "core", SWAP)]
    return pieces


def sequence_of(r):
    z = lax.axis_index("z")
    core = lax.axis_index("core")
    other = core if r % 2 == 0 else 1 - core
    return 2 * lax.rem(z + 4 - r // 2, 4) + other


def trade(blocks):
    done = [blocks[0]]
    for r in range(1, 8):
        o, f = r // 2, r % 2
        pairs = [(2 * z + c, 2 * ((z - o) % 4) + (c ^ f)) for z in range(4) for c in range(2)]
        done.append(lax.ppermute(blocks[r], DP, pairs))
    return done


def halve(keep, give):
    got = lax.ppermute(give, "core", SWAP)
    return [(keep[o].astype(F32) + got[o].astype(F32)).astype(BF) for o in range(4)]


def exchange(s):
    return [
        s[0],
        lax.ppermute(s[1], "z", DOWN),
        lax.ppermute(s[2], "z", ACROSS),
        lax.ppermute(s[3], "z", UP),
    ]


def total_of(terms):
    return sum(t.astype(F32) for t in terms)


def swap_all(x, axes):
    return lax.all_to_all(x, axes, split_axis=0, concat_axis=0, tiled=True)


def rms_back(d_gained, unit, inv_scale, gain):
    d_unit = d_gained * gain
    return inv_scale * (d_unit - unit * jnp.mean(d_unit * unit, axis=-1, keepdims=True))


def inv_rms(x):
    return lax.rsqrt(jnp.mean(x * x, axis=-1, keepdims=True) + EPSILON)


def dot(spec, a, b):
    return jnp.einsum(spec, a, b, preferred_element_type=F32)


def mm(a, b, ca=1, cb=0):
    return lax.dot_general(a, b, (((ca,), (cb,)), ((), ())), preferred_element_type=F32)


def sender_of(r):
    z = lax.axis_index("z")
    core = lax.axis_index("core")
    other = core if r % 2 == 0 else 1 - core
    return 2 * lax.rem(z + r // 2, 4) + other


def pack_kernel(gu_ref, down_ref, mark_ref, *refs):
    outs, held = refs[:8], refs[8]
    keep = lax.broadcasted_iota(jnp.int32, (8, PAD), 1) < UNITS
    for part, (ref, base) in enumerate(((gu_ref, 0), (gu_ref, FF), (down_ref, 0))):
        for p in range(4):
            at = base + 2 * UNITS * p
            both = ref[:, at : at + 2 * UNITS].astype(F32)
            turned = pltpu.roll(both, UNITS, 1)
            held[2 * p, :, PAD * part : PAD * part + PAD] = jnp.where(keep, both[:, :PAD], 0.0)
            held[2 * p + 1, :, PAD * part : PAD * part + PAD] = jnp.where(keep, turned[:, :PAD], 0.0)
    for r in range(8):
        outs[r][...] = held[sequence_of(r)].astype(BF)


def pack(w_gu, w_down, mark):
    return pl.pallas_call(
        pack_kernel,
        out_shape=[shape((8, 3 * PAD))] * 8,
        in_specs=[VMEM] * 2 + [ANY],
        out_specs=[VMEM] * 8,
        scratch_shapes=[pltpu.VMEM((8, 8, 3 * PAD), F32)],
        compiler_params=params(16),
        cost_estimate=pl.CostEstimate(flops=0, bytes_accessed=1 << 19, transcendentals=0),
    )(w_gu, w_down, mark)


def merge_kernel(*refs):
    for r in range(8):
        refs[8][sender_of(r)] = refs[r][...]


def merge(blocks):
    return pl.pallas_call(
        merge_kernel,
        out_shape=shape((8, 8, 3 * PAD)),
        in_specs=[VMEM] * 8,
        out_specs=VMEM,
        compiler_params=params(16),
        cost_estimate=pl.CostEstimate(flops=0, bytes_accessed=1 << 19, transcendentals=0),
    )(*blocks)


def part_kernel(g_ref, *outs):
    for r in range(8):
        outs[r][...] = g_ref[sequence_of(r)]


def part(g):
    return pl.pallas_call(
        part_kernel,
        out_shape=[shape((8, 3 * PAD))] * 8,
        in_specs=[VMEM],
        out_specs=[VMEM] * 8,
        compiler_params=params(16),
        cost_estimate=pl.CostEstimate(flops=0, bytes_accessed=1 << 19, transcendentals=0),
    )(g)


def unpack_kernel(*refs):
    gu_ref, down_ref, held = refs[8:]
    for r in range(8):
        held[sender_of(r)] = refs[r][...].astype(F32)
    first = lax.broadcasted_iota(jnp.int32, (8, 2 * UNITS), 1) < UNITS
    blank = jnp.zeros((8, 2 * UNITS - PAD), F32)
    for k, (ref, base) in enumerate(((gu_ref, 0), (gu_ref, FF), (down_ref, 0))):
        for p in range(4):
            a, b = [
                jnp.concatenate([held[2 * p + i, :, PAD * k : PAD * k + PAD], blank], axis=1)
                for i in range(2)
            ]
            at = base + 2 * UNITS * p
            ref[:, at : at + 2 * UNITS] = jnp.where(first, a, pltpu.roll(b, UNITS, 1))


def unpack(blocks):
    return pl.pallas_call(
        unpack_kernel,
        out_shape=[shape((8, 2 * FF), F32), shape((8, FF), F32)],
        in_specs=[VMEM] * 8,
        out_specs=[VMEM] * 2,
        scratch_shapes=[pltpu.VMEM((8, 8, 3 * PAD), F32)],
        compiler_params=params(16),
        cost_estimate=pl.CostEstimate(flops=0, bytes_accessed=1 << 20, transcendentals=0),
    )(*blocks)


def lanes_of(rows):
    return lax.broadcasted_iota(jnp.int32, (rows, 128), 1)


def head_mean(v, lane):
    low = jnp.sum(jnp.where(lane < 64, v, 0.0), axis=-1, keepdims=True)
    high = jnp.sum(jnp.where(lane < 64, 0.0, v), axis=-1, keepdims=True)
    return jnp.where(lane < 64, low, high) * (1.0 / HD)


def partner(v, lane):
    return jnp.where((lane & 32) == 0, pltpu.roll(v, 96, 1), pltpu.roll(v, 32, 1))


def trig(tables, orders_ref, b):
    cf, sf, cn, sn = tables
    s = lax.axis_index(SEQ)
    sign = jnp.where((lanes_of(SPAN) & 32) == 0, -1.0, 1.0)
    cos, sin = [], []
    for k in range(2):
        span = orders_ref[b, 2 * s + k]
        c, d = cf[pl.ds(span, 1), :], sf[pl.ds(span, 1), :]
        cos.append(c * cn[...] - d * sn[...])
        sin.append((d * cn[...] + c * sn[...]) * sign)
    return jnp.concatenate(cos), jnp.concatenate(sin)


def project_kernel(*refs):
    toks = refs[:8]
    got_ref, a_gain, qk_gain, wout_ref, orders_ref = refs[8:13]
    tables = refs[13:17]
    send_ref, x_ref, h_ref, mixed_ref, w_ref = refs[17:]
    step = pl.program_id(0)

    @pl.when(step == 0)
    def _():
        got = got_ref[:, 0:16, :].astype(F32)
        w_ref[:, :128] = got[:, :8].reshape(1024, 128).astype(BF)
        w_ref[:, 128:] = got[:, 8:].reshape(1024, 128).astype(BF)
        for i in range(16):
            send_ref[i, 192:256, :] = wout_ref[...]

    lane = lanes_of(128)
    low = lane < 64
    def sequence(r):
        x = toks[r][...]
        at = slice(128 * (r % 2), 128 * (r % 2) + 128)
        x_ref[at, :] = x
        x = x.astype(F32)
        h = (x * inv_rms(x) * a_gain[...]).astype(BF)
        h_ref[at, :] = h
        mixed = mm(h, w_ref[...])
        mixed_ref[at, :] = mixed
        b = sequence_of(r)
        cos, sin = trig(tables, orders_ref, b)

        def turned(v, gain):
            g = v * lax.rsqrt(head_mean(v * v, lane) + EPSILON) * gain
            return g * cos + partner(g, lane) * sin

        q = turned(mixed[:, :128], qk_gain[0:1, :])
        kv = jnp.where(low, turned(mixed[:, 128:], qk_gain[1:2, :]), mixed[:, 128:]).astype(BF)
        flip = pltpu.roll(q, 64, 1)
        l64 = low[:64]
        send_ref[2 * b, 0:128, :] = kv
        send_ref[2 * b + 1, 0:128, :] = kv
        send_ref[2 * b, 128:192, :] = jnp.where(l64, q[:64], flip[64:]).astype(BF)
        send_ref[2 * b + 1, 128:192, :] = jnp.where(l64, flip[:64], q[64:]).astype(BF)

    for o in range(4):

        @pl.when(step == o)
        def _():
            sequence(2 * o)
            sequence(2 * o + 1)


def project(toks, got, a_gain, qk_gain, w_out, orders, tables):
    return pl.pallas_call(
        project_kernel,
        out_shape=[
            shape((16, 256, 128)),
            shape((1024, 1024)),
            shape((1024, 1024)),
            shape((1024, 256), F32),
            shape((1024, 256)),
        ],
        grid=(4,),
        in_specs=[whole(128, 1024)] * 8
        + [whole(128, 24, 128), whole(1, 1024), whole(2, 128), whole(64, 128), SMEM]
        + [whole(SPANS, 128)] * 2
        + [whole(SPAN, 128)] * 2,
        out_specs=[
            whole(16, 256, 128),
            rows(256, 1024),
            rows(256, 1024),
            rows(256, 256),
            whole(1024, 256),
        ],
        compiler_params=params(40),
        cost_estimate=slow(10**11),
    )(*toks, got, a_gain, qk_gain, w_out, orders, *tables)


def attend_kernel(
    qkv_ref, orders_ref, send_ref, q_ref, kv_ref, ot_ref, lse_ref, wout_ref, kvt, osc, wout32
):
    for s in range(16):
        block = qkv_ref[s, 192:256, :].astype(F32)
        for j in range(8):
            wout32[8 * s : 8 * s + 8, 128 * j : 128 * j + 128] = block[8 * j : 8 * j + 8]
    wout_ref[...] = wout32[...].astype(BF)
    b = lax.axis_index(SEQ) // 2
    l64 = lanes_of(64) < 64
    for i in range(32):
        at = pl.multiple_of(orders_ref[b, i] * 64, 64)
        kv_ref[pl.ds(at, 64), :] = qkv_ref[i // 2, 64 * (i % 2) : 64 * (i % 2) + 64, :]
        block = qkv_ref[i // 2, 128:192, :].astype(F32)
        if i % 2:
            block = pltpu.roll(block, 64, 1)
        q_ref[pl.ds(at, 64), :] = jnp.where(l64, block * HD**-0.5, 0.0).astype(BF)
    kvt[...] = kv_ref[...].T
    after = lax.broadcasted_iota(jnp.int32, (256, 256), 0) > lax.broadcasted_iota(
        jnp.int32, (256, 256), 1
    )
    for i in range(8):
        n = 256 * i
        q = q_ref[n : n + 256, :]
        near = jnp.where(after, -1e30, mm(kv_ref[n : n + 256, :], q, 1, 1))
        top = jnp.max(near, axis=0, keepdims=True)
        if i:
            far = mm(kv_ref[:n, :], q, 1, 1)
            top = jnp.maximum(top, jnp.max(far, axis=0, keepdims=True))
        near = jnp.exp(near - top)
        total = jnp.sum(near, axis=0, keepdims=True)
        o = mm(kvt[:, n : n + 256], near.astype(BF))
        if i:
            far = jnp.exp(far - top)
            total = total + jnp.sum(far, axis=0, keepdims=True)
            o = o + mm(kvt[:, :n], far.astype(BF))
        o = o / total
        ot_ref[:, n : n + 256] = o[64:]
        lse_ref[:, n : n + 256] = top + jnp.log(total)
        osc[n : n + 256, :] = o.T
    for i in range(16):
        a = osc[pl.ds(pl.multiple_of(orders_ref[b, 2 * i] * 64, 64), 64), :]
        c = osc[pl.ds(pl.multiple_of(orders_ref[b, 2 * i + 1] * 64, 64), 64), :]
        send_ref[i] = jnp.where(l64, pltpu.roll(a, 64, 1), c).astype(BF)


def attend(qkv, orders):
    return pl.pallas_call(
        attend_kernel,
        out_shape=[
            shape((16, 64, 128)),
            shape((2048, 128)),
            shape((2048, 128)),
            shape((64, 2048), F32),
            shape((1, 2048), F32),
            shape((128, 1024)),
        ],
        in_specs=[VMEM, SMEM],
        out_specs=[VMEM] * 6,
        scratch_shapes=[
            pltpu.VMEM((128, 2048), BF),
            pltpu.VMEM((2048, 128), F32),
            pltpu.VMEM((128, 1024), F32),
        ],
        compiler_params=params(40),
        cost_estimate=pl.CostEstimate(flops=2 * 2048 * 2048 * 128, bytes_accessed=4 << 20, transcendentals=2 << 20),
    )(qkv, orders)


def attend_back_kernel(
    got_ref, q_ref, kv_ref, ot_ref, lse_ref, orders_ref, send_ref, do, kvt, dkv, dqs
):
    b = lax.axis_index(SEQ) // 2
    l64 = lanes_of(64) < 64
    for i in range(32):
        at = pl.multiple_of(orders_ref[b, i] * 64, 64)
        block = got_ref[i // 2].astype(F32)
        if i % 2 == 0:
            block = pltpu.roll(block, 64, 1)
        do[pl.ds(at, 64), :] = jnp.where(l64, 0.0, block)
    kvt[...] = kv_ref[...].T
    before = lax.broadcasted_iota(jnp.int32, (256, 256), 0) <= lax.broadcasted_iota(
        jnp.int32, (256, 256), 1
    )
    dkv[...] = jnp.zeros_like(dkv)
    for i in range(8):
        n = 256 * i
        q = q_ref[n : n + 256, :]
        d32 = do[n : n + 256, :]
        d = d32.astype(BF)
        lse = lse_ref[:, n : n + 256]
        delta = jnp.sum(ot_ref[:, n : n + 256] * d32.T[64:], axis=0, keepdims=True)
        dq = None
        for lo, hi in ((n, n + 256), (0, n)):
            if lo == hi:
                continue
            keys = kv_ref[lo:hi, :]
            p = jnp.exp(mm(keys, q, 1, 1) - lse)
            if lo:
                p = jnp.where(before, p, 0.0)
            elif hi == 256 and n == 0:
                p = jnp.where(before, p, 0.0)
            ds = (p * (mm(keys, d, 1, 1) - delta)).astype(BF)
            dkv[lo:hi, :] += mm(ds, q) + mm(p.astype(BF), d)
            term = mm(kvt[:, lo:hi], ds)
            dq = term if dq is None else dq + term
        dqs[n : n + 256, :] = (dq * HD**-0.5).T
    for i in range(16):
        at = pl.multiple_of(orders_ref[b, 2 * i] * 64, 64)
        bt = pl.multiple_of(orders_ref[b, 2 * i + 1] * 64, 64)
        send_ref[i, 0:64, :] = dkv[pl.ds(at, 64), :].astype(BF)
        send_ref[i, 64:128, :] = dkv[pl.ds(bt, 64), :].astype(BF)
        send_ref[i, 128:192, :] = jnp.where(
            l64, dqs[pl.ds(at, 64), :], pltpu.roll(dqs[pl.ds(bt, 64), :], 64, 1)
        ).astype(BF)


def attend_back(got, q, kv, ot, lse, orders):
    return pl.pallas_call(
        attend_back_kernel,
        out_shape=shape((16, 192, 128)),
        in_specs=[VMEM] * 5 + [SMEM],
        out_specs=VMEM,
        scratch_shapes=[
            pltpu.VMEM((2048, 128), F32),
            pltpu.VMEM((128, 2048), BF),
            pltpu.VMEM((2048, 128), F32),
            pltpu.VMEM((2048, 128), F32),
        ],
        compiler_params=params(40),
        cost_estimate=pl.CostEstimate(flops=5 * 2048 * 2048 * 128, bytes_accessed=4 << 20, transcendentals=2 << 20),
    )(got, q, kv, ot, lse, orders)


def heads_of(pair, r):
    l64 = lanes_of(64) < 64
    b = sequence_of(r)
    a = pair[2 * b].astype(F32)
    c = pair[2 * b + 1].astype(F32)
    return jnp.concatenate(
        [jnp.where(l64, a, pltpu.roll(c, 64, 1)), jnp.where(l64, pltpu.roll(a, 64, 1), c)]
    )


def feed_kernel(*refs):
    douts, atn, wouts = refs[:8], refs[8:16], refs[16:24]
    x_ref, f_gain, w_ref = refs[24:27]
    keep_ref, give_ref, x1_ref, h2_ref, act_ref, dgu_ref, gf_ref, wo = refs[27:]
    step = pl.program_id(0)

    @pl.when(step == 0)
    def _():
        for r in range(8):
            wo[128 * r : 128 * r + 128, :] = wouts[r][...]
        gf_ref[...] = jnp.zeros_like(gf_ref)

    def block(o):
        cols = [
            jnp.concatenate([heads_of(atn[k], 2 * o), heads_of(atn[k], 2 * o + 1)]).astype(BF)
            for k in range(8)
        ]
        attn = jnp.concatenate(cols, axis=1)
        x1 = x_ref[...].astype(F32) + mm(attn, wo[...])
        if o == 0:
            x1_ref[...] = x1[:128]
        n2 = x1 * inv_rms(x1)
        h2 = (n2 * f_gain[...]).astype(BF)
        h2_ref[...] = h2
        gate_up = mm(h2, w_ref[:, : 2 * PAD])
        gate, upper = gate_up[:, :PAD], gate_up[:, PAD:]
        sigma = jax.nn.sigmoid(gate)
        swish = gate * sigma
        act_ref[...] = (swish * upper).astype(BF)
        d = jnp.concatenate([douts[2 * o][...], douts[2 * o + 1][...]])
        d_act = mm(d, w_ref[:, 2 * PAD :]).astype(BF).astype(F32)
        d_gate = d_act * upper * (sigma * (1.0 + gate * (1.0 - sigma)))
        dgu_ref[:, :PAD] = d_gate.astype(BF)
        dgu_ref[:, PAD:] = (d_act * swish).astype(BF)
        d_h2 = mm(dgu_ref[...], w_ref[:, : 2 * PAD], 1, 1)
        gf_ref[...] += jnp.sum(d_h2 * n2, axis=0, keepdims=True)
        keep_ref[0] = d_h2[:128].astype(BF)
        give_ref[0] = d_h2[128:].astype(BF)

    for o in range(4):
        pl.when(step == o)(lambda o=o: block(o))


QUARTER = pl.BlockSpec((1, 128, 1024), lambda i: (i, 0, 0))


def feed(douts, attns, wouts, x, f_gain, w_ff):
    return pl.pallas_call(
        feed_kernel,
        out_shape=[
            shape((4, 128, 1024)),
            shape((4, 128, 1024)),
            shape((128, 1024), F32),
            shape((1024, 1024)),
            shape((1024, PAD)),
            shape((1024, 2 * PAD)),
            shape((1, 1024), F32),
        ],
        grid=(4,),
        in_specs=[whole(128, 1024)] * 8
        + [whole(16, 64, 128)] * 8
        + [whole(128, 1024)] * 8
        + [rows(256, 1024), whole(1, 1024), whole(1024, 3 * PAD)],
        out_specs=[
            QUARTER,
            QUARTER,
            whole(128, 1024),
            rows(256, 1024),
            rows(256, PAD),
            rows(256, 2 * PAD),
            whole(1, 1024),
        ],
        scratch_shapes=[pltpu.VMEM((1024, 1024), BF)],
        compiler_params=params(56),
        cost_estimate=pl.CostEstimate(flops=2 * 1024 * 1024 * 4224, bytes_accessed=20 << 20, transcendentals=1 << 20),
    )(*douts, *attns, *wouts, x, f_gain, w_ff)


def feed_grad_kernel(*refs):
    douts = refs[:8]
    h2_ref, act_ref, dgu_ref, w_ref, mark_ref = refs[8:13]
    g_ref, keep_ref, give_ref, ht, dt = refs[13:]
    for r in range(8):
        dt[:, 128 * r : 128 * r + 128] = douts[r][...].T
    ht[...] = h2_ref[...].T
    for p in range(4):
        for n, part_of in enumerate(((ht, dgu_ref), (dt, act_ref))):
            left, right = part_of
            at = slice(2 * PAD * n, 2 * PAD * n + right.shape[1])
            g = mm(left[256 * p : 256 * p + 256, :], right[...])
            for s in range(16):
                pair = [g[8 * s : 8 * s + 8], g[128 + 8 * s : 136 + 8 * s]]
                g_ref[s, 16 * p : 16 * p + 16, at] = jnp.concatenate(pair).astype(BF)
    for o in range(4):
        out = mm(act_ref[256 * o : 256 * o + 256, :], w_ref[...], 1, 1)
        keep_ref[o] = out[:128].astype(BF)
        give_ref[o] = out[128:].astype(BF)


def feed_grad(douts, h2, act, d_gu, w_ff, mark):
    return pl.pallas_call(
        feed_grad_kernel,
        out_shape=[shape((16, 64, 3 * PAD)), shape((4, 128, 1024)), shape((4, 128, 1024))],
        grid=(1,),
        in_specs=[whole(128, 1024)] * 8
        + [whole(1024, 1024), whole(1024, PAD), whole(1024, 2 * PAD)]
        + [pl.BlockSpec((1024, PAD), lambda i: (0, 2)), ANY],
        out_specs=[whole(16, 64, 3 * PAD), whole(4, 128, 1024), whole(4, 128, 1024)],
        scratch_shapes=[pltpu.VMEM((1024, 1024), BF), pltpu.VMEM((1024, 1024), BF)],
        compiler_params=params(56),
        cost_estimate=pl.CostEstimate(flops=2 * 1024 * 1024 * 2560, bytes_accessed=18 << 20, transcendentals=0),
    )(*douts, h2, act, d_gu, w_ff, mark)


def unproject_kernel(*refs):
    x_ref, back_ref, mixed_ref, w_ref, qk_gain, orders_ref = refs[:6]
    tables = refs[6:10]
    keep_ref, give_ref, dm_ref, ga_ref, gqk_ref = refs[10:]
    lane = lanes_of(128)
    low = lane < 64
    step = pl.program_id(0)

    @pl.when(step == 0)
    def _():
        ga_ref[...] = jnp.zeros_like(ga_ref)
        gqk_ref[...] = jnp.zeros_like(gqk_ref)

    def sequence(r):
        b = sequence_of(r)
        cos, sin = trig(tables, orders_ref, b)
        at = slice(128 * (r % 2), 128 * (r % 2) + 128)
        mixed = mixed_ref[at, :]
        u = back_ref[2 * b].astype(F32)
        v = back_ref[2 * b + 1].astype(F32)
        d_kv = u[:128] + v[:128]
        u, v = u[128:], v[128:]
        l64 = low[:64]
        d_q = jnp.concatenate(
            [
                jnp.where(l64, u, pltpu.roll(v, 64, 1)),
                jnp.where(l64, pltpu.roll(u, 64, 1), v),
            ]
        )

        def turned_back(d, raw, gain):
            scale = lax.rsqrt(head_mean(raw * raw, lane) + EPSILON)
            unit = raw * scale
            g = d * cos - partner(d, lane) * sin
            e = g * gain
            grad = jnp.sum(g * unit, axis=0, keepdims=True)
            return scale * (e - unit * head_mean(e * unit, lane)), grad

        dq_raw, grad_q = turned_back(d_q, mixed[:, :128], qk_gain[0:1, :])
        dk_raw, grad_k = turned_back(d_kv, mixed[:, 128:], qk_gain[1:2, :])
        gqk_ref[0:1, :] += grad_q
        gqk_ref[1:2, :] += grad_k
        dm = jnp.concatenate([dq_raw, jnp.where(low, dk_raw, d_kv)], axis=1).astype(BF)
        dm_ref[at, :] = dm
        d_h = mm(dm, w_ref[...], 1, 1)
        x = x_ref[at, :].astype(F32)
        ga_ref[...] += jnp.sum(d_h * (x * inv_rms(x)), axis=0, keepdims=True)
        (give_ref if r % 2 else keep_ref)[0] = d_h.astype(BF)

    for o in range(4):

        @pl.when(step == o)
        def _():
            sequence(2 * o)
            sequence(2 * o + 1)


def unproject(x, back, mixed, w, qk_gain, orders, tables):
    return pl.pallas_call(
        unproject_kernel,
        out_shape=[
            shape((4, 128, 1024)),
            shape((4, 128, 1024)),
            shape((1024, 256)),
            shape((1, 1024), F32),
            shape((2, 128), F32),
        ],
        grid=(4,),
        in_specs=[
            rows(256, 1024),
            whole(16, 192, 128),
            rows(256, 256),
            whole(1024, 256),
            whole(2, 128),
            SMEM,
        ]
        + [whole(SPANS, 128)] * 2
        + [whole(SPAN, 128)] * 2,
        out_specs=[QUARTER, QUARTER, rows(256, 256), whole(1, 1024), whole(2, 128)],
        compiler_params=params(40),
        cost_estimate=pl.CostEstimate(flops=2 * 1024 * 1024 * 256, bytes_accessed=8 << 20, transcendentals=0),
    )(far(x), back, far(mixed), far(w), qk_gain, orders, *tables)


def own_kernel(t0, t1, t2, t3, x1_ref, f_gain, d_ref, *refs):
    wouts, dx_ref, send_ref = refs[:8], refs[8], refs[9]
    d_h2 = sum(t[...].astype(F32) for t in (t0, t1, t2, t3))
    x1 = x1_ref[...]
    scale = inv_rms(x1)
    d_x1 = d_ref[...].astype(F32) + rms_back(d_h2, x1 * scale, scale, f_gain[...])
    dx_ref[...] = d_x1
    branch = d_x1.astype(BF)
    for j in range(8):
        send_ref[j, 128:256, :] = branch[:, 128 * j : 128 * j + 128]
    l64 = lanes_of(64) < 64
    for k in range(8):
        j = sequence_of(k)
        d_attn = mm(branch, wouts[k][...], 1, 1)
        top, low = d_attn[:64], d_attn[64:]
        send_ref[j, 0:64, :] = jnp.where(l64, top, pltpu.roll(low, 64, 1)).astype(BF)
        send_ref[j, 64:128, :] = jnp.where(l64, pltpu.roll(top, 64, 1), low).astype(BF)


def own_tokens(terms, x1, f_gain, d_out, wouts):
    return pl.pallas_call(
        own_kernel,
        out_shape=[shape((128, 1024), F32), shape((8, 256, 128))],
        in_specs=[VMEM] * 15,
        out_specs=[VMEM] * 2,
        compiler_params=params(32),
        cost_estimate=slow(10**11),
    )(*terms, x1, f_gain, d_out, *wouts)


def out_grad_kernel(*refs):
    atn, got_ref, out_ref = refs[:8], refs[8], refs[9]
    d = jnp.concatenate([got_ref[sequence_of(r), 128:256, :] for r in range(8)])
    for k in range(8):
        attn = jnp.concatenate([heads_of(atn[k], r) for r in range(8)])
        grad = mm(attn.T.astype(BF), d)
        out_ref[pl.ds(16 * sequence_of(k), 16)] = grad.reshape(16, 8, 128)


def out_grad(attns, got):
    return pl.pallas_call(
        out_grad_kernel,
        out_shape=shape((128, 8, 128), F32),
        in_specs=[VMEM] * 9,
        out_specs=VMEM,
        compiler_params=params(32),
        cost_estimate=pl.CostEstimate(flops=2 * 128 * 1024 * 1024, bytes_accessed=3 << 20, transcendentals=0),
    )(*attns, got)


def last_kernel(h_ref, dm_ref, gout_ref, gains_ref, out_ref, ht):
    for c in range(4):
        ht[256 * c : 256 * c + 256, :] = h_ref[:, 256 * c : 256 * c + 256].T
    g = mm(ht[...], dm_ref[...])
    a = g[:, :128].reshape(128, 8, 128)
    b = g[:, 128:].reshape(128, 8, 128)
    out_ref[:, 0:16, :] = jnp.concatenate([a, b], axis=1).astype(BF)
    out_ref[:, 16:32, :] = jnp.concatenate([gout_ref[...], gains_ref[...]], axis=1).astype(BF)


def last_pack(h, d_mixed, g_out, gains):
    return pl.pallas_call(
        last_kernel,
        out_shape=shape((128, 32, 128)),
        in_specs=[VMEM] * 4,
        out_specs=VMEM,
        scratch_shapes=[pltpu.VMEM((1024, 1024), BF)],
        compiler_params=params(32),
        cost_estimate=pl.CostEstimate(flops=2 * 256 * 1024 * 1024, bytes_accessed=5 << 20, transcendentals=0),
    )(h, d_mixed, g_out, gains)


def on_device(tokens, w_qkv, w_out, w_gu, w_down, gains, span_order, d_out):
    tables = [jnp.asarray(a) for a in lane_tables()]

    wq = w_qkv[:, :1024].reshape(8, 8, 128)
    wkv = jnp.concatenate(
        [w_qkv[:, 1024:1536].reshape(8, 8, 64), w_qkv[:, 1536:].reshape(8, 8, 64)], axis=-1
    )
    extra = jnp.concatenate([gains, span_order[0].astype(BF), jnp.zeros((79,), BF)])
    pay = jnp.concatenate(
        [wq.transpose(1, 0, 2), wkv.transpose(1, 0, 2), jnp.broadcast_to(extra, (8, 8, 128))], axis=1
    )
    pay = jnp.broadcast_to(pay[:, None], (8, 16, 24, 128)).reshape(128, 24, 128)
    got = swap_all(pay, ALL)
    toks = gather_dp(tokens[0])

    packed = pack(w_gu, w_down, toks[4])
    w_ff = lax.all_gather(merge(trade(packed)), SEQ, axis=1, tiled=False)
    w_ff = w_ff.reshape(1024, 3 * PAD)

    gain_all = got[:, 16, :17].reshape(2176).astype(F32)
    orders = got.reshape(8, 16, 24, 128)[:, 0, 16, 17:49].astype(jnp.int32)
    a_gain = gain_all[None, :1024]
    f_gain = gain_all[None, 1024:2048]
    q_gain, k_gain = gain_all[2048:2112], gain_all[2112:]
    qk_gain = jnp.stack([jnp.concatenate([q_gain, q_gain]), jnp.concatenate([k_gain, k_gain])])
    w_out_pay = w_out.reshape(8, 8, 128).transpose(1, 0, 2).reshape(64, 128)

    send, x_all, h, mixed, w_j = project(toks, got, a_gain, qk_gain, w_out_pay, orders, tables)
    qkv = swap_all(send, SEQ)
    douts = gather_dp(d_out[0])
    o_send, q_s, kv_s, ot, lse, w_out_j = attend(qkv, orders)
    wouts = gather_dp(w_out_j)
    o_got = swap_all(o_send, SEQ)
    attns = gather_dp(o_got)
    d_keep, d_give, x1, h2, act, d_gu, gf_part = feed(
        douts, attns, wouts, x_all, f_gain, w_ff
    )
    s_h2 = halve(d_keep, d_give)
    d_x1, d_send = own_tokens(exchange(s_h2), x1, f_gain, d_out[0], wouts)

    g_ff, out_keep, out_give = feed_grad(douts, h2, act, d_gu, w_ff, s_h2[0])
    g_ff = lax.psum_scatter(g_ff.reshape(1024, 3 * PAD), SEQ, scatter_dimension=0, tiled=True)

    d_got = swap_all(d_send, DP)
    d_o = swap_all(d_got[:, :128].reshape(16, 64, 128), SEQ)
    d_o, out_keep, out_give = lax.optimization_barrier((d_o, out_keep, out_give))
    terms = exchange(halve(out_keep, out_give))
    back = swap_all(attend_back(d_o, q_s, kv_s, ot, lse, orders), SEQ)
    g_out_part = out_grad(attns, d_got)
    back, terms, g_out_part = lax.optimization_barrier((back, terms, g_out_part))
    result = x1 + total_of(terms)
    h_keep, h_give, d_mixed, ga_part, gqk_part = unproject(
        x_all, back, mixed, w_j, qk_gain, orders, tables
    )
    s_h = halve(h_keep, h_give)
    h_terms = exchange(s_h)
    gq_part = gqk_part[0, :64] + gqk_part[0, 64:]
    g_gain = jnp.concatenate([ga_part[0], gf_part[0], gq_part, gqk_part[1, :64]]).reshape(128, 17)
    gain_hi = g_gain.astype(BF).astype(F32)
    gain_rows = jnp.concatenate([gain_hi, g_gain - gain_hi, jnp.zeros((128, 94), F32)], axis=1)
    gain_rows = jnp.broadcast_to(gain_rows[:, None], (128, 8, 128))
    last = swap_all(last_pack(h, d_mixed, g_out_part, gain_rows), ALL)
    g_gu, g_down = unpack(trade(part(g_ff.reshape(8, 8, 3 * PAD))))
    last, g_gu, g_down, *h_terms = lax.optimization_barrier((last, g_gu, g_down, *h_terms))
    last = last.astype(F32)
    d_h = total_of(h_terms)
    x = tokens[0].astype(F32)
    r1 = inv_rms(x)
    d_tokens = d_x1 + rms_back(d_h, x * r1, r1, a_gain)

    g_gains = jnp.sum(last[:, 24, :17] + last[:, 24, 17:34], axis=0)
    last = jnp.sum(last.reshape(8, 16, 32, 128), axis=1)
    g_out = last[:, 16:24].transpose(1, 0, 2).reshape(8, 1024)
    g_qkv = jnp.concatenate(
        [
            last[:, :8].transpose(1, 0, 2).reshape(8, 1024),
            last[:, 8:16, :64].transpose(1, 0, 2).reshape(8, 512),
            last[:, 8:16, 64:].transpose(1, 0, 2).reshape(8, 512),
        ],
        axis=1,
    )
    return (
        result.astype(BF)[None],
        d_tokens[None],
        g_qkv,
        g_out,
        g_gu,
        g_down,
        g_gains,
    )


def solution(mesh):
    split = Mesh(mesh.devices.reshape(4, 2, 4, 4), ALL)
    return jax.shard_map(
        on_device,
        mesh=split,
        in_specs=(
            P(DP, SEQ, None),
            P(ALL, None),
            P(ALL, None),
            P(ALL, None),
            P(ALL, None),
            P(ALL),
            P(DP, None),
            P(DP, SEQ, None),
        ),
        out_specs=(
            P(DP, SEQ, None),
            P(DP, SEQ, None),
            P(ALL, None),
            P(ALL, None),
            P(ALL, None),
            P(ALL, None),
            P(ALL),
        ),
        check_vma=False,
    )
```

```python
import jax
import jax.numpy as jnp
import numpy as np
from jax import lax
from jax.experimental import pallas as pl
from jax.experimental.pallas import tpu as pltpu
from jax.sharding import Mesh
from jax.sharding import PartitionSpec as P

D = 1024
H = 16
KVH = 8
HD = 64
FF = 4608
LOC = 128
SPAN = 64
SPANS = 32
DP = ("z", "core")
SEQ = ("x", "y")
ALL = ("z", "core", "x", "y")
UNITS = FF // 8
PAD = 640

EPSILON = 1e-05
THETA = 1000000.0
BF = jnp.bfloat16
F32 = jnp.float32

UP = [(i, (i + 1) % 4) for i in range(4)]
DOWN = [(i, (i - 1) % 4) for i in range(4)]
ACROSS = [(i, (i + 2) % 4) for i in range(4)]
SWAP = [(0, 1), (1, 0)]


def params(mb):
    return pltpu.CompilerParams(vmem_limit_bytes=mb * 2**20)


def shape(dims, kind=BF):
    return pltpu.HBM(dims, kind)


SMEM = pl.BlockSpec(memory_space=pltpu.SMEM)
VMEM = pl.BlockSpec(memory_space=pltpu.VMEM)
ANY = pl.BlockSpec(memory_space=pl.ANY)


def whole(*dims):
    return pl.BlockSpec(dims, lambda i: (0,) * len(dims))


def rows(n, width):
    return pl.BlockSpec((n, width), lambda i: (i, 0))


def slow(x):
    return pl.CostEstimate(flops=x, bytes_accessed=0, transcendentals=0)


def far(x):
    return pltpu.with_memory_space_constraint(x, pltpu.HBM)


def lane_tables():
    freqs = THETA ** (-(np.arange(HD // 2) * 2.0 / HD))
    lanes = freqs[np.arange(128) % (HD // 2)]
    far = (np.arange(SPANS) * SPAN)[:, None] * lanes[None]
    near = np.arange(SPAN)[:, None] * lanes[None]
    return [f(a).astype(np.float32) for a in (far, near) for f in (np.cos, np.sin)]


def gather_dp(x):
    a = lax.ppermute(x, "z", UP)
    b = lax.ppermute(x, "z", DOWN)
    c = lax.ppermute(x, "z", ACROSS)
    pieces = []
    for v in (x, a, c, b):
        pieces += [v, lax.ppermute(v, "core", SWAP)]
    return pieces


def sequence_of(r):
    z = lax.axis_index("z")
    core = lax.axis_index("core")
    other = core if r % 2 == 0 else 1 - core
    return 2 * lax.rem(z + 4 - r // 2, 4) + other


def trade(blocks):
    done = [blocks[0]]
    for r in range(1, 8):
        o, f = r // 2, r % 2
        pairs = [(2 * z + c, 2 * ((z - o) % 4) + (c ^ f)) for z in range(4) for c in range(2)]
        done.append(lax.ppermute(blocks[r], DP, pairs))
    return done


def halve(keep, give):
    got = lax.ppermute(give, "core", SWAP)
    return [(keep[o].astype(F32) + got[o].astype(F32)).astype(BF) for o in range(4)]


def exchange(s):
    return [
        s[0],
        lax.ppermute(s[1], "z", DOWN),
        lax.ppermute(s[2], "z", ACROSS),
        lax.ppermute(s[3], "z", UP),
    ]


def total_of(terms):
    return sum(t.astype(F32) for t in terms)


def swap_all(x, axes):
    return lax.all_to_all(x, axes, split_axis=0, concat_axis=0, tiled=True)


def rms_back(d_gained, unit, inv_scale, gain):
    d_unit = d_gained * gain
    return inv_scale * (d_unit - unit * jnp.mean(d_unit * unit, axis=-1, keepdims=True))


def inv_rms(x):
    return lax.rsqrt(jnp.mean(x * x, axis=-1, keepdims=True) + EPSILON)


def dot(spec, a, b):
    return jnp.einsum(spec, a, b, preferred_element_type=F32)


def mm(a, b, ca=1, cb=0):
    return lax.dot_general(a, b, (((ca,), (cb,)), ((), ())), preferred_element_type=F32)


def sender_of(r):
    z = lax.axis_index("z")
    core = lax.axis_index("core")
    other = core if r % 2 == 0 else 1 - core
    return 2 * lax.rem(z + r // 2, 4) + other


WIDE = 3 * PAD + 384


def pack_kernel(gu_ref, down_ref, qkv_ref, gains_ref, order_ref, *refs):
    outs, held, extra = refs[:8], refs[8], refs[9]
    keep = lax.broadcasted_iota(jnp.int32, (8, PAD), 1) < UNITS
    for part, (ref, base) in enumerate(((gu_ref, 0), (gu_ref, FF), (down_ref, 0))):
        for p in range(4):
            at = base + 2 * UNITS * p
            both = ref[:, at : at + 2 * UNITS].astype(F32)
            turned = pltpu.roll(both, UNITS, 1)
            held[2 * p, :, PAD * part : PAD * part + PAD] = jnp.where(keep, both[:, :PAD], 0.0)
            held[2 * p + 1, :, PAD * part : PAD * part + PAD] = jnp.where(keep, turned[:, :PAD], 0.0)
    extra[...] = jnp.zeros_like(extra)
    extra[0:1, 0:17] = gains_ref[...].astype(F32)
    extra[1:2, 0:32] = order_ref[...].astype(F32)
    low = lanes_of(8) < 64
    at = 3 * PAD
    for j in range(8):
        held[j, :, at : at + 128] = qkv_ref[:, 128 * j : 128 * j + 128].astype(F32)
        k = qkv_ref[:, 1024 + 128 * (j // 2) : 1152 + 128 * (j // 2)].astype(F32)
        v = qkv_ref[:, 1536 + 128 * (j // 2) : 1664 + 128 * (j // 2)].astype(F32)
        if j % 2:
            k = pltpu.roll(k, 64, 1)
        else:
            v = pltpu.roll(v, 64, 1)
        held[j, :, at + 128 : at + 256] = jnp.where(low, k, v)
        held[j, :, at + 256 : at + 384] = extra[...]
    for r in range(8):
        outs[r][...] = held[sequence_of(r)].astype(BF)


def pack(w_gu, w_down, w_qkv, gains, order):
    return pl.pallas_call(
        pack_kernel,
        out_shape=[shape((8, WIDE))] * 8,
        in_specs=[VMEM] * 5,
        out_specs=[VMEM] * 8,
        scratch_shapes=[pltpu.VMEM((8, 8, WIDE), F32), pltpu.VMEM((8, 128), F32)],
        compiler_params=params(16),
        cost_estimate=slow(10**9),
    )(w_gu, w_down, w_qkv, gains, order)


def merge_kernel(*refs):
    ff_ref, seq_ref, held = refs[9:]
    at = 3 * PAD
    for r in range(8):
        j = sender_of(r)
        got = refs[r][...]
        ff_ref[j] = got[:, :at]
        rest = got[:, at:].astype(F32)
        row = pl.multiple_of(8 * j, 8)
        held[pl.ds(row, 8), :] = rest[:, :128]
        held[pl.ds(row + 64, 8), :] = rest[:, 128:256]
        held[pl.ds(128 + j, 1), :] = rest[0:1, 256:]
        held[pl.ds(136 + j, 1), :] = rest[1:2, 256:]
    for s in range(16):
        seq_ref[s] = held[...].astype(BF)


def merge(blocks, wait):
    return pl.pallas_call(
        merge_kernel,
        out_shape=[shape((8, 8, 3 * PAD)), shape((16, 144, 128))],
        in_specs=[VMEM] * 8 + [ANY],
        out_specs=[VMEM] * 2,
        scratch_shapes=[pltpu.VMEM((144, 128), F32)],
        compiler_params=params(16),
        cost_estimate=slow(10**9),
    )(*blocks, wait)


def part_kernel(g_ref, *outs):
    for r in range(8):
        outs[r][...] = g_ref[sequence_of(r)]


def part(g):
    return pl.pallas_call(
        part_kernel,
        out_shape=[shape((8, 3 * PAD))] * 8,
        in_specs=[VMEM],
        out_specs=[VMEM] * 8,
        compiler_params=params(16),
        cost_estimate=pl.CostEstimate(flops=0, bytes_accessed=1 << 19, transcendentals=0),
    )(g)


def unpack_kernel(*refs):
    gu_ref, down_ref, held = refs[8:]
    for r in range(8):
        held[sender_of(r)] = refs[r][...].astype(F32)
    first = lax.broadcasted_iota(jnp.int32, (8, 2 * UNITS), 1) < UNITS
    blank = jnp.zeros((8, 2 * UNITS - PAD), F32)
    for k, (ref, base) in enumerate(((gu_ref, 0), (gu_ref, FF), (down_ref, 0))):
        for p in range(4):
            a, b = [
                jnp.concatenate([held[2 * p + i, :, PAD * k : PAD * k + PAD], blank], axis=1)
                for i in range(2)
            ]
            at = base + 2 * UNITS * p
            ref[:, at : at + 2 * UNITS] = jnp.where(first, a, pltpu.roll(b, UNITS, 1))


def unpack(blocks):
    return pl.pallas_call(
        unpack_kernel,
        out_shape=[shape((8, 2 * FF), F32), shape((8, FF), F32)],
        in_specs=[VMEM] * 8,
        out_specs=[VMEM] * 2,
        scratch_shapes=[pltpu.VMEM((8, 8, 3 * PAD), F32)],
        compiler_params=params(16),
        cost_estimate=pl.CostEstimate(flops=0, bytes_accessed=1 << 20, transcendentals=0),
    )(*blocks)


def lanes_of(rows):
    return lax.broadcasted_iota(jnp.int32, (rows, 128), 1)


def head_mean(v, lane):
    low = jnp.sum(jnp.where(lane < 64, v, 0.0), axis=-1, keepdims=True)
    high = jnp.sum(jnp.where(lane < 64, 0.0, v), axis=-1, keepdims=True)
    return jnp.where(lane < 64, low, high) * (1.0 / HD)


def partner(v, lane):
    return jnp.where((lane & 32) == 0, pltpu.roll(v, 96, 1), pltpu.roll(v, 32, 1))


def trig(tables, orders_ref, b):
    cf, sf, cn, sn = tables
    s = lax.axis_index(SEQ)
    sign = jnp.where((lanes_of(SPAN) & 32) == 0, -1.0, 1.0)
    cos, sin = [], []
    for k in range(2):
        span = orders_ref[b, 2 * s + k]
        c, d = cf[pl.ds(span, 1), :], sf[pl.ds(span, 1), :]
        cos.append(c * cn[...] - d * sn[...])
        sin.append((d * cn[...] + c * sn[...]) * sign)
    return jnp.concatenate(cos), jnp.concatenate(sin)


def project_kernel(*refs):
    toks = refs[:8]
    got_ref, a_gain, qk_gain, wout_ref, orders_ref = refs[8:13]
    tables = refs[13:17]
    send_ref, x_ref, h_ref, mixed_ref, w_ref, w32 = refs[17:]
    step = pl.program_id(0)

    @pl.when(step == 0)
    def _():
        for s in range(16):
            got = got_ref[s, 0:128, :].astype(F32)
            for j in range(8):
                at = 128 * j + 8 * s
                w32[at : at + 8, :128] = got[8 * j : 8 * j + 8]
                w32[at : at + 8, 128:] = got[64 + 8 * j : 72 + 8 * j]
        w_ref[...] = w32[...].astype(BF)
        for i in range(16):
            send_ref[i, 192:256, :] = wout_ref[...]

    lane = lanes_of(128)
    low = lane < 64
    def sequence(r):
        x = toks[r][...]
        at = slice(128 * (r % 2), 128 * (r % 2) + 128)
        x_ref[at, :] = x
        x = x.astype(F32)
        h = (x * inv_rms(x) * a_gain[...]).astype(BF)
        h_ref[at, :] = h
        mixed = mm(h, w_ref[...])
        mixed_ref[at, :] = mixed
        b = sequence_of(r)
        cos, sin = trig(tables, orders_ref, b)

        def turned(v, gain):
            g = v * lax.rsqrt(head_mean(v * v, lane) + EPSILON) * gain
            return g * cos + partner(g, lane) * sin

        q = turned(mixed[:, :128], qk_gain[0:1, :])
        kv = jnp.where(low, turned(mixed[:, 128:], qk_gain[1:2, :]), mixed[:, 128:]).astype(BF)
        flip = pltpu.roll(q, 64, 1)
        l64 = low[:64]
        send_ref[2 * b, 0:128, :] = kv
        send_ref[2 * b + 1, 0:128, :] = kv
        send_ref[2 * b, 128:192, :] = jnp.where(l64, q[:64], flip[64:]).astype(BF)
        send_ref[2 * b + 1, 128:192, :] = jnp.where(l64, flip[:64], q[64:]).astype(BF)

    for o in range(4):

        @pl.when(step == o)
        def _():
            sequence(2 * o)
            sequence(2 * o + 1)


def project(toks, got, a_gain, qk_gain, w_out, orders, tables):
    return pl.pallas_call(
        project_kernel,
        out_shape=[
            shape((16, 256, 128)),
            shape((1024, 1024)),
            shape((1024, 1024)),
            shape((1024, 256), F32),
            shape((1024, 256)),
        ],
        grid=(4,),
        in_specs=[whole(128, 1024)] * 8
        + [whole(16, 144, 128), whole(1, 1024), whole(2, 128), whole(64, 128), SMEM]
        + [whole(SPANS, 128)] * 2
        + [whole(SPAN, 128)] * 2,
        out_specs=[
            whole(16, 256, 128),
            rows(256, 1024),
            rows(256, 1024),
            rows(256, 256),
            whole(1024, 256),
        ],
        scratch_shapes=[pltpu.VMEM((1024, 256), F32)],
        compiler_params=params(40),
        cost_estimate=slow(10**11),
    )(*toks, got, a_gain, qk_gain, w_out, orders, *tables)


def attend_kernel(
    qkv_ref, orders_ref, send_ref, q_ref, kv_ref, ot_ref, lse_ref, wout_ref, kvt, osc, wout32
):
    for s in range(16):
        block = qkv_ref[s, 192:256, :].astype(F32)
        for j in range(8):
            wout32[8 * s : 8 * s + 8, 128 * j : 128 * j + 128] = block[8 * j : 8 * j + 8]
    wout_ref[...] = wout32[...].astype(BF)
    b = lax.axis_index(SEQ) // 2
    l64 = lanes_of(64) < 64
    for i in range(32):
        at = pl.multiple_of(orders_ref[b, i] * 64, 64)
        kv_ref[pl.ds(at, 64), :] = qkv_ref[i // 2, 64 * (i % 2) : 64 * (i % 2) + 64, :]
        block = qkv_ref[i // 2, 128:192, :].astype(F32)
        if i % 2:
            block = pltpu.roll(block, 64, 1)
        q_ref[pl.ds(at, 64), :] = jnp.where(l64, block * HD**-0.5, 0.0).astype(BF)
    kvt[...] = kv_ref[...].T
    after = lax.broadcasted_iota(jnp.int32, (256, 256), 0) > lax.broadcasted_iota(
        jnp.int32, (256, 256), 1
    )
    for i in range(8):
        n = 256 * i
        q = q_ref[n : n + 256, :]
        near = jnp.where(after, -1e30, mm(kv_ref[n : n + 256, :], q, 1, 1))
        top = jnp.max(near, axis=0, keepdims=True)
        if i:
            far = mm(kv_ref[:n, :], q, 1, 1)
            top = jnp.maximum(top, jnp.max(far, axis=0, keepdims=True))
        near = jnp.exp(near - top)
        total = jnp.sum(near, axis=0, keepdims=True)
        o = mm(kvt[:, n : n + 256], near.astype(BF))
        if i:
            far = jnp.exp(far - top)
            total = total + jnp.sum(far, axis=0, keepdims=True)
            o = o + mm(kvt[:, :n], far.astype(BF))
        o = o / total
        ot_ref[:, n : n + 256] = o[64:]
        lse_ref[:, n : n + 256] = top + jnp.log(total)
        osc[n : n + 256, :] = o.T
    for i in range(16):
        a = osc[pl.ds(pl.multiple_of(orders_ref[b, 2 * i] * 64, 64), 64), :]
        c = osc[pl.ds(pl.multiple_of(orders_ref[b, 2 * i + 1] * 64, 64), 64), :]
        send_ref[i] = jnp.where(l64, pltpu.roll(a, 64, 1), c).astype(BF)


def attend(qkv, orders):
    return pl.pallas_call(
        attend_kernel,
        out_shape=[
            shape((16, 64, 128)),
            shape((2048, 128)),
            shape((2048, 128)),
            shape((64, 2048), F32),
            shape((1, 2048), F32),
            shape((128, 1024)),
        ],
        in_specs=[VMEM, SMEM],
        out_specs=[VMEM] * 6,
        scratch_shapes=[
            pltpu.VMEM((128, 2048), BF),
            pltpu.VMEM((2048, 128), F32),
            pltpu.VMEM((128, 1024), F32),
        ],
        compiler_params=params(40),
        cost_estimate=pl.CostEstimate(flops=2 * 2048 * 2048 * 128, bytes_accessed=4 << 20, transcendentals=2 << 20),
    )(qkv, orders)


def attend_back_kernel(
    got_ref, q_ref, kv_ref, ot_ref, lse_ref, orders_ref, send_ref, do, kvt, dkv, dqs
):
    b = lax.axis_index(SEQ) // 2
    l64 = lanes_of(64) < 64
    for i in range(32):
        at = pl.multiple_of(orders_ref[b, i] * 64, 64)
        block = got_ref[i // 2].astype(F32)
        if i % 2 == 0:
            block = pltpu.roll(block, 64, 1)
        do[pl.ds(at, 64), :] = jnp.where(l64, 0.0, block)
    kvt[...] = kv_ref[...].T
    before = lax.broadcasted_iota(jnp.int32, (256, 256), 0) <= lax.broadcasted_iota(
        jnp.int32, (256, 256), 1
    )
    dkv[...] = jnp.zeros_like(dkv)
    for i in range(8):
        n = 256 * i
        q = q_ref[n : n + 256, :]
        d32 = do[n : n + 256, :]
        d = d32.astype(BF)
        lse = lse_ref[:, n : n + 256]
        delta = jnp.sum(ot_ref[:, n : n + 256] * d32.T[64:], axis=0, keepdims=True)
        dq = None
        for lo, hi in ((n, n + 256), (0, n)):
            if lo == hi:
                continue
            keys = kv_ref[lo:hi, :]
            p = jnp.exp(mm(keys, q, 1, 1) - lse)
            if lo:
                p = jnp.where(before, p, 0.0)
            elif hi == 256 and n == 0:
                p = jnp.where(before, p, 0.0)
            ds = (p * (mm(keys, d, 1, 1) - delta)).astype(BF)
            dkv[lo:hi, :] += mm(ds, q) + mm(p.astype(BF), d)
            term = mm(kvt[:, lo:hi], ds)
            dq = term if dq is None else dq + term
        dqs[n : n + 256, :] = (dq * HD**-0.5).T
    for i in range(16):
        at = pl.multiple_of(orders_ref[b, 2 * i] * 64, 64)
        bt = pl.multiple_of(orders_ref[b, 2 * i + 1] * 64, 64)
        send_ref[i, 0:64, :] = dkv[pl.ds(at, 64), :].astype(BF)
        send_ref[i, 64:128, :] = dkv[pl.ds(bt, 64), :].astype(BF)
        send_ref[i, 128:192, :] = jnp.where(
            l64, dqs[pl.ds(at, 64), :], pltpu.roll(dqs[pl.ds(bt, 64), :], 64, 1)
        ).astype(BF)


def attend_back(got, q, kv, ot, lse, orders):
    return pl.pallas_call(
        attend_back_kernel,
        out_shape=shape((16, 192, 128)),
        in_specs=[VMEM] * 5 + [SMEM],
        out_specs=VMEM,
        scratch_shapes=[
            pltpu.VMEM((2048, 128), F32),
            pltpu.VMEM((128, 2048), BF),
            pltpu.VMEM((2048, 128), F32),
            pltpu.VMEM((2048, 128), F32),
        ],
        compiler_params=params(40),
        cost_estimate=pl.CostEstimate(flops=5 * 2048 * 2048 * 128, bytes_accessed=4 << 20, transcendentals=2 << 20),
    )(got, q, kv, ot, lse, orders)


def heads_of(pair, r):
    l64 = lanes_of(64) < 64
    b = sequence_of(r)
    a = pair[2 * b].astype(F32)
    c = pair[2 * b + 1].astype(F32)
    return jnp.concatenate(
        [jnp.where(l64, a, pltpu.roll(c, 64, 1)), jnp.where(l64, pltpu.roll(a, 64, 1), c)]
    )


def feed_kernel(*refs):
    douts, atn, wouts = refs[:8], refs[8:16], refs[16:24]
    x_ref, f_gain, w_ref = refs[24:27]
    keep_ref, give_ref, x1_ref, h2_ref, act_ref, dgu_ref, gf_ref, wo = refs[27:]
    step = pl.program_id(0)

    @pl.when(step == 0)
    def _():
        for r in range(8):
            wo[128 * r : 128 * r + 128, :] = wouts[r][...]
        gf_ref[...] = jnp.zeros_like(gf_ref)

    def block(o):
        cols = [
            jnp.concatenate([heads_of(atn[k], 4 * o + i) for i in range(4)]).astype(BF)
            for k in range(8)
        ]
        attn = jnp.concatenate(cols, axis=1)
        x1 = x_ref[...].astype(F32) + mm(attn, wo[...])
        if o == 0:
            x1_ref[...] = x1[:128]
        n2 = x1 * inv_rms(x1)
        h2 = (n2 * f_gain[...]).astype(BF)
        h2_ref[...] = h2
        gate_up = mm(h2, w_ref[:, : 2 * PAD])
        gate, upper = gate_up[:, :PAD], gate_up[:, PAD:]
        sigma = jax.nn.sigmoid(gate)
        swish = gate * sigma
        act_ref[...] = (swish * upper).astype(BF)
        d = jnp.concatenate([douts[4 * o + i][...] for i in range(4)])
        d_act = mm(d, w_ref[:, 2 * PAD :]).astype(BF).astype(F32)
        d_gate = d_act * upper * (sigma * (1.0 + gate * (1.0 - sigma)))
        dgu_ref[:, :PAD] = d_gate.astype(BF)
        dgu_ref[:, PAD:] = (d_act * swish).astype(BF)
        d_h2 = mm(dgu_ref[...], w_ref[:, : 2 * PAD], 1, 1)
        gf_ref[...] += jnp.sum(d_h2 * n2, axis=0, keepdims=True)
        for i in range(2):
            keep_ref[i] = d_h2[256 * i : 256 * i + 128].astype(BF)
            give_ref[i] = d_h2[256 * i + 128 : 256 * i + 256].astype(BF)

    for o in range(2):
        pl.when(step == o)(lambda o=o: block(o))


QUARTER = pl.BlockSpec((1, 128, 1024), lambda i: (i, 0, 0))
HALF = pl.BlockSpec((2, 128, 1024), lambda i: (i, 0, 0))


def feed(douts, attns, wouts, x, f_gain, w_ff):
    return pl.pallas_call(
        feed_kernel,
        out_shape=[
            shape((4, 128, 1024)),
            shape((4, 128, 1024)),
            shape((128, 1024), F32),
            shape((1024, 1024)),
            shape((1024, PAD)),
            shape((1024, 2 * PAD)),
            shape((1, 1024), F32),
        ],
        grid=(2,),
        in_specs=[whole(128, 1024)] * 8
        + [whole(16, 64, 128)] * 8
        + [whole(128, 1024)] * 8
        + [rows(512, 1024), whole(1, 1024), whole(1024, 3 * PAD)],
        out_specs=[
            HALF,
            HALF,
            whole(128, 1024),
            rows(512, 1024),
            rows(512, PAD),
            rows(512, 2 * PAD),
            whole(1, 1024),
        ],
        scratch_shapes=[pltpu.VMEM((1024, 1024), BF)],
        compiler_params=params(56),
        cost_estimate=pl.CostEstimate(flops=2 * 1024 * 1024 * 4224, bytes_accessed=20 << 20, transcendentals=1 << 20),
    )(*douts, *attns, *wouts, x, f_gain, w_ff)


def feed_grad_kernel(*refs):
    douts = refs[:8]
    h2_ref, act_ref, dgu_ref, w_ref = refs[8:12]
    g_ref, keep_ref, give_ref, ht, dt = refs[12:]
    for r in range(8):
        dt[:, 128 * r : 128 * r + 128] = douts[r][...].T
    ht[...] = h2_ref[...].T
    for p in range(4):
        for n, part_of in enumerate(((ht, dgu_ref), (dt, act_ref))):
            left, right = part_of
            at = slice(2 * PAD * n, 2 * PAD * n + right.shape[1])
            g = mm(left[256 * p : 256 * p + 256, :], right[...])
            for s in range(16):
                pair = [g[8 * s : 8 * s + 8], g[128 + 8 * s : 136 + 8 * s]]
                g_ref[s, 16 * p : 16 * p + 16, at] = jnp.concatenate(pair).astype(BF)
    for o in range(4):
        out = mm(act_ref[256 * o : 256 * o + 256, :], w_ref[...], 1, 1)
        keep_ref[o] = out[:128].astype(BF)
        give_ref[o] = out[128:].astype(BF)


def feed_grad(douts, h2, act, d_gu, w_ff):
    return pl.pallas_call(
        feed_grad_kernel,
        out_shape=[shape((16, 64, 3 * PAD)), shape((4, 128, 1024)), shape((4, 128, 1024))],
        grid=(1,),
        in_specs=[whole(128, 1024)] * 8
        + [whole(1024, 1024), whole(1024, PAD), whole(1024, 2 * PAD)]
        + [pl.BlockSpec((1024, PAD), lambda i: (0, 2))],
        out_specs=[whole(16, 64, 3 * PAD), whole(4, 128, 1024), whole(4, 128, 1024)],
        scratch_shapes=[pltpu.VMEM((1024, 1024), BF), pltpu.VMEM((1024, 1024), BF)],
        compiler_params=params(56),
        cost_estimate=pl.CostEstimate(flops=2 * 1024 * 1024 * 2560, bytes_accessed=18 << 20, transcendentals=0),
    )(*douts, h2, act, d_gu, w_ff)


def unproject_kernel(*refs):
    x_ref, back_ref, mixed_ref, w_ref, qk_gain, orders_ref = refs[:6]
    tables = refs[6:10]
    keep_ref, give_ref, dm_ref, ga_ref, gqk_ref = refs[10:]
    lane = lanes_of(128)
    low = lane < 64
    step = pl.program_id(0)

    @pl.when(step == 0)
    def _():
        ga_ref[...] = jnp.zeros_like(ga_ref)
        gqk_ref[...] = jnp.zeros_like(gqk_ref)

    def sequence(r):
        b = sequence_of(r)
        cos, sin = trig(tables, orders_ref, b)
        at = slice(128 * (r % 2), 128 * (r % 2) + 128)
        mixed = mixed_ref[at, :]
        u = back_ref[2 * b].astype(F32)
        v = back_ref[2 * b + 1].astype(F32)
        d_kv = u[:128] + v[:128]
        u, v = u[128:], v[128:]
        l64 = low[:64]
        d_q = jnp.concatenate(
            [
                jnp.where(l64, u, pltpu.roll(v, 64, 1)),
                jnp.where(l64, pltpu.roll(u, 64, 1), v),
            ]
        )

        def turned_back(d, raw, gain):
            scale = lax.rsqrt(head_mean(raw * raw, lane) + EPSILON)
            unit = raw * scale
            g = d * cos - partner(d, lane) * sin
            e = g * gain
            grad = jnp.sum(g * unit, axis=0, keepdims=True)
            return scale * (e - unit * head_mean(e * unit, lane)), grad

        dq_raw, grad_q = turned_back(d_q, mixed[:, :128], qk_gain[0:1, :])
        dk_raw, grad_k = turned_back(d_kv, mixed[:, 128:], qk_gain[1:2, :])
        gqk_ref[0:1, :] += grad_q
        gqk_ref[1:2, :] += grad_k
        dm = jnp.concatenate([dq_raw, jnp.where(low, dk_raw, d_kv)], axis=1).astype(BF)
        dm_ref[at, :] = dm
        d_h = mm(dm, w_ref[...], 1, 1)
        x = x_ref[at, :].astype(F32)
        ga_ref[...] += jnp.sum(d_h * (x * inv_rms(x)), axis=0, keepdims=True)
        (give_ref if r % 2 else keep_ref)[0] = d_h.astype(BF)

    for o in range(4):

        @pl.when(step == o)
        def _():
            sequence(2 * o)
            sequence(2 * o + 1)


def unproject(x, back, mixed, w, qk_gain, orders, tables):
    return pl.pallas_call(
        unproject_kernel,
        out_shape=[
            shape((4, 128, 1024)),
            shape((4, 128, 1024)),
            shape((1024, 256)),
            shape((1, 1024), F32),
            shape((2, 128), F32),
        ],
        grid=(4,),
        in_specs=[
            rows(256, 1024),
            whole(16, 192, 128),
            rows(256, 256),
            whole(1024, 256),
            whole(2, 128),
            SMEM,
        ]
        + [whole(SPANS, 128)] * 2
        + [whole(SPAN, 128)] * 2,
        out_specs=[QUARTER, QUARTER, rows(256, 256), whole(1, 1024), whole(2, 128)],
        compiler_params=params(40),
        cost_estimate=pl.CostEstimate(flops=2 * 1024 * 1024 * 256, bytes_accessed=8 << 20, transcendentals=0),
    )(far(x), back, far(mixed), far(w), qk_gain, orders, *tables)


def own_kernel(t0, t1, t2, t3, x1_ref, f_gain, d_ref, *refs):
    wouts, dx_ref, send_ref = refs[:8], refs[8], refs[9]
    d_h2 = sum(t[...].astype(F32) for t in (t0, t1, t2, t3))
    x1 = x1_ref[...]
    scale = inv_rms(x1)
    d_x1 = d_ref[...].astype(F32) + rms_back(d_h2, x1 * scale, scale, f_gain[...])
    dx_ref[...] = d_x1
    branch = d_x1.astype(BF)
    for j in range(8):
        send_ref[j, 128:256, :] = branch[:, 128 * j : 128 * j + 128]
    l64 = lanes_of(64) < 64
    for k in range(8):
        j = sequence_of(k)
        d_attn = mm(branch, wouts[k][...], 1, 1)
        top, low = d_attn[:64], d_attn[64:]
        send_ref[j, 0:64, :] = jnp.where(l64, top, pltpu.roll(low, 64, 1)).astype(BF)
        send_ref[j, 64:128, :] = jnp.where(l64, pltpu.roll(top, 64, 1), low).astype(BF)


def own_tokens(terms, x1, f_gain, d_out, wouts):
    return pl.pallas_call(
        own_kernel,
        out_shape=[shape((128, 1024), F32), shape((8, 256, 128))],
        in_specs=[VMEM] * 15,
        out_specs=[VMEM] * 2,
        compiler_params=params(32),
        cost_estimate=slow(10**11),
    )(*terms, x1, f_gain, d_out, *wouts)


def out_grad_kernel(*refs):
    atn, got_ref, out_ref = refs[:8], refs[8], refs[9]
    d = jnp.concatenate([got_ref[sequence_of(r), 128:256, :] for r in range(8)])
    for k in range(8):
        attn = jnp.concatenate([heads_of(atn[k], r) for r in range(8)])
        grad = mm(attn.T.astype(BF), d)
        out_ref[pl.ds(16 * sequence_of(k), 16)] = grad.reshape(16, 8, 128)


def out_grad(attns, got):
    return pl.pallas_call(
        out_grad_kernel,
        out_shape=shape((128, 8, 128), F32),
        in_specs=[VMEM] * 9,
        out_specs=VMEM,
        compiler_params=params(32),
        cost_estimate=pl.CostEstimate(flops=2 * 128 * 1024 * 1024, bytes_accessed=3 << 20, transcendentals=0),
    )(*attns, got)


def last_kernel(h_ref, dm_ref, gout_ref, gains_ref, out_ref, ht):
    for c in range(4):
        ht[256 * c : 256 * c + 256, :] = h_ref[:, 256 * c : 256 * c + 256].T
    g = mm(ht[...], dm_ref[...])
    a = g[:, :128].reshape(128, 8, 128)
    b = g[:, 128:].reshape(128, 8, 128)
    out_ref[:, 0:16, :] = jnp.concatenate([a, b], axis=1).astype(BF)
    out_ref[:, 16:32, :] = jnp.concatenate([gout_ref[...], gains_ref[...]], axis=1).astype(BF)


def last_pack(h, d_mixed, g_out, gains):
    return pl.pallas_call(
        last_kernel,
        out_shape=shape((128, 32, 128)),
        in_specs=[VMEM] * 4,
        out_specs=VMEM,
        scratch_shapes=[pltpu.VMEM((1024, 1024), BF)],
        compiler_params=params(32),
        cost_estimate=slow(10**9),
    )(far(h), far(d_mixed), g_out, gains)


def finish_kernel(last_ref, t0, t1, t2, t3, x_ref, a_gain, dx_ref, dtok_ref, gqkv_ref, gout_ref, gains_ref):
    d_h = sum(t[...].astype(F32) for t in (t0, t1, t2, t3))
    x = x_ref[...].astype(F32)
    scale = inv_rms(x)
    dtok_ref[...] = dx_ref[...] + rms_back(d_h, x * scale, scale, a_gain[...])
    low = lanes_of(8) < 64
    gains = jnp.zeros((8, 128), F32)
    for p in range(4):
        kv = []
        for j in (2 * p, 2 * p + 1):
            acc = jnp.sum(last_ref[16 * j : 16 * j + 16].astype(F32), axis=0)
            gqkv_ref[:, 128 * j : 128 * j + 128] = acc[0:8]
            kv.append(acc[8:16])
            gout_ref[:, 128 * j : 128 * j + 128] = acc[16:24]
            gains = gains + acc[24:32]
        at = 1024 + 128 * p
        gqkv_ref[:, at : at + 128] = jnp.where(low, kv[0], pltpu.roll(kv[1], 64, 1))
        gqkv_ref[:, at + 512 : at + 640] = jnp.where(low, pltpu.roll(kv[0], 64, 1), kv[1])
    gains_ref[...] = gains + pltpu.roll(gains, 128 - 17, 1)


def finish(last, terms, x, a_gain, d_x1):
    return pl.pallas_call(
        finish_kernel,
        out_shape=[
            shape((128, 1024), F32),
            shape((8, 2048), F32),
            shape((8, 1024), F32),
            shape((8, 128), F32),
        ],
        in_specs=[VMEM] * 8,
        out_specs=[VMEM] * 4,
        compiler_params=params(32),
        cost_estimate=slow(10**9),
    )(last, *terms, x, a_gain, d_x1)


def on_device(tokens, w_qkv, w_out, w_gu, w_down, gains, span_order, d_out):
    tables = [jnp.asarray(a) for a in lane_tables()]

    toks = gather_dp(tokens[0])
    packed = pack(far(w_gu), far(w_down), far(w_qkv), gains[None], span_order)
    ff_pay, seq_pay = merge(trade(packed), toks[4])
    got = swap_all(seq_pay, SEQ)
    w_ff = lax.all_gather(ff_pay, SEQ, axis=1, tiled=False).reshape(1024, 3 * PAD)

    gain_all = got[:, 128:136, :17].transpose(1, 0, 2).reshape(2176).astype(F32)
    orders = got[0, 136:144, :32].astype(jnp.int32)
    a_gain = gain_all[None, :1024]
    f_gain = gain_all[None, 1024:2048]
    q_gain, k_gain = gain_all[2048:2112], gain_all[2112:]
    qk_gain = jnp.stack([jnp.concatenate([q_gain, q_gain]), jnp.concatenate([k_gain, k_gain])])
    w_out_pay = w_out.reshape(8, 8, 128).transpose(1, 0, 2).reshape(64, 128)

    send, x_all, h, mixed, w_j = project(toks, got, a_gain, qk_gain, w_out_pay, orders, tables)
    qkv = swap_all(send, SEQ)
    douts = gather_dp(d_out[0])
    o_send, q_s, kv_s, ot, lse, w_out_j = attend(qkv, orders)
    wouts = gather_dp(w_out_j)
    o_got = swap_all(o_send, SEQ)
    attns = gather_dp(o_got)
    d_keep, d_give, x1, h2, act, d_gu, gf_part = feed(
        douts, attns, wouts, x_all, f_gain, w_ff
    )
    s_h2 = halve(d_keep, d_give)
    h2, *s_h2 = lax.optimization_barrier((h2, *s_h2))
    d_x1, d_send = own_tokens(exchange(s_h2), x1, f_gain, d_out[0], wouts)

    g_ff, out_keep, out_give = feed_grad(douts, h2, act, d_gu, w_ff)
    g_ff = lax.psum_scatter(g_ff.reshape(1024, 3 * PAD), SEQ, scatter_dimension=0, tiled=True)

    d_got = swap_all(d_send, DP)
    d_o = swap_all(d_got[:, :128].reshape(16, 64, 128), SEQ)
    d_o, out_keep, out_give = lax.optimization_barrier((d_o, out_keep, out_give))
    terms = exchange(halve(out_keep, out_give))
    back = swap_all(attend_back(d_o, q_s, kv_s, ot, lse, orders), SEQ)
    g_out_part = out_grad(attns, d_got)
    back, terms, g_out_part = lax.optimization_barrier((back, terms, g_out_part))
    result = x1 + total_of(terms)
    h_keep, h_give, d_mixed, ga_part, gqk_part = unproject(
        x_all, back, mixed, w_j, qk_gain, orders, tables
    )
    s_h = halve(h_keep, h_give)
    gq_part = gqk_part[0, :64] + gqk_part[0, 64:]
    g_gain = jnp.concatenate([ga_part[0], gf_part[0], gq_part, gqk_part[1, :64]]).reshape(128, 17)
    gain_hi = g_gain.astype(BF).astype(F32)
    gain_rows = jnp.concatenate([gain_hi, g_gain - gain_hi, jnp.zeros((128, 94), F32)], axis=1)
    gain_rows = jnp.broadcast_to(gain_rows[:, None], (128, 8, 128))
    gain_rows, *s_h = lax.optimization_barrier((gain_rows, *s_h))
    h_terms = exchange(s_h)
    last = swap_all(last_pack(h, d_mixed, g_out_part, gain_rows), ALL)
    g_gu, g_down = unpack(trade(part(g_ff.reshape(8, 8, 3 * PAD))))
    last, g_gu, g_down, *h_terms = lax.optimization_barrier((last, g_gu, g_down, *h_terms))
    d_tokens, g_qkv, g_out, g_gains = finish(last, h_terms, tokens[0], a_gain, d_x1)
    return (
        result.astype(BF)[None],
        d_tokens[None],
        g_qkv,
        g_out,
        g_gu,
        g_down,
        g_gains[0, :17],
    )


def solution(mesh):
    split = Mesh(mesh.devices.reshape(4, 2, 4, 4), ALL)
    return jax.shard_map(
        on_device,
        mesh=split,
        in_specs=(
            P(DP, SEQ, None),
            P(ALL, None),
            P(ALL, None),
            P(ALL, None),
            P(ALL, None),
            P(ALL),
            P(DP, None),
            P(DP, SEQ, None),
        ),
        out_specs=(
            P(DP, SEQ, None),
            P(DP, SEQ, None),
            P(ALL, None),
            P(ALL, None),
            P(ALL, None),
            P(ALL, None),
            P(ALL),
        ),
        check_vma=False,
    )
```

```python
import jax
import jax.numpy as jnp
import numpy as np
from jax import lax
from jax.experimental import pallas as pl
from jax.experimental.pallas import tpu as pltpu
from jax.sharding import Mesh
from jax.sharding import PartitionSpec as P

D = 1024
H = 16
KVH = 8
HD = 64
FF = 4608
LOC = 128
SPAN = 64
SPANS = 32
DP = ("z", "core")
SEQ = ("x", "y")
ALL = ("z", "core", "x", "y")
UNITS = FF // 8
PAD = 640

EPSILON = 1e-05
THETA = 1000000.0
BF = jnp.bfloat16
F32 = jnp.float32

UP = [(i, (i + 1) % 4) for i in range(4)]
DOWN = [(i, (i - 1) % 4) for i in range(4)]
ACROSS = [(i, (i + 2) % 4) for i in range(4)]
SWAP = [(0, 1), (1, 0)]


def params(mb):
    return pltpu.CompilerParams(vmem_limit_bytes=mb * 2**20)


def shape(dims, kind=BF):
    return pltpu.HBM(dims, kind)


def near(dims, kind=BF):
    return jax.ShapeDtypeStruct(dims, kind)


SMEM = pl.BlockSpec(memory_space=pltpu.SMEM)
VMEM = pl.BlockSpec(memory_space=pltpu.VMEM)
ANY = pl.BlockSpec(memory_space=pl.ANY)


def whole(*dims):
    return pl.BlockSpec(dims, lambda i: (0,) * len(dims))


def rows(n, width):
    return pl.BlockSpec((n, width), lambda i: (i, 0))


def slow(x):
    return pl.CostEstimate(flops=x, bytes_accessed=0, transcendentals=0)


def far(x):
    return pltpu.with_memory_space_constraint(x, pltpu.HBM)


def lane_tables():
    freqs = THETA ** (-(np.arange(HD // 2) * 2.0 / HD))
    lanes = freqs[np.arange(128) % (HD // 2)]
    far = (np.arange(SPANS) * SPAN)[:, None] * lanes[None]
    near = np.arange(SPAN)[:, None] * lanes[None]
    return [f(a).astype(np.float32) for a in (far, near) for f in (np.cos, np.sin)]


def gather_dp(x):
    a = lax.ppermute(x, "z", UP)
    b = lax.ppermute(x, "z", DOWN)
    c = lax.ppermute(x, "z", ACROSS)
    pieces = []
    for v in (x, a, c, b):
        pieces += [v, lax.ppermute(v, "core", SWAP)]
    return pieces


def sequence_of(r):
    z = lax.axis_index("z")
    core = lax.axis_index("core")
    other = core if r % 2 == 0 else 1 - core
    return 2 * lax.rem(z + 4 - r // 2, 4) + other


def trade(blocks):
    done = [blocks[0]]
    for r in range(1, 8):
        o, f = r // 2, r % 2
        pairs = [(2 * z + c, 2 * ((z - o) % 4) + (c ^ f)) for z in range(4) for c in range(2)]
        done.append(lax.ppermute(blocks[r], DP, pairs))
    return done


def halve_kernel(keep_ref, got_ref, *outs):
    for o in range(4):
        outs[o][...] = (keep_ref[o].astype(F32) + got_ref[o].astype(F32)).astype(BF)


def halve(keep, give):
    got = lax.ppermute(give, "core", SWAP)
    return pl.pallas_call(
        halve_kernel,
        out_shape=[shape((128, 1024))] * 4,
        in_specs=[VMEM] * 2,
        out_specs=[VMEM] * 4,
        compiler_params=params(16),
        cost_estimate=pl.CostEstimate(flops=0, bytes_accessed=3 << 20, transcendentals=0),
    )(keep, got)


def exchange(s):
    return [
        s[0],
        lax.ppermute(s[1], "z", DOWN),
        lax.ppermute(s[2], "z", ACROSS),
        lax.ppermute(s[3], "z", UP),
    ]


def total_of(terms):
    return sum(t.astype(F32) for t in terms)


def swap_all(x, axes):
    return lax.all_to_all(x, axes, split_axis=0, concat_axis=0, tiled=True)


def rms_back(d_gained, unit, inv_scale, gain):
    d_unit = d_gained * gain
    return inv_scale * (d_unit - unit * jnp.mean(d_unit * unit, axis=-1, keepdims=True))


def inv_rms(x):
    return lax.rsqrt(jnp.mean(x * x, axis=-1, keepdims=True) + EPSILON)


def dot(spec, a, b):
    return jnp.einsum(spec, a, b, preferred_element_type=F32)


def mm(a, b, ca=1, cb=0):
    return lax.dot_general(a, b, (((ca,), (cb,)), ((), ())), preferred_element_type=F32)


def sender_of(r):
    z = lax.axis_index("z")
    core = lax.axis_index("core")
    other = core if r % 2 == 0 else 1 - core
    return 2 * lax.rem(z + r // 2, 4) + other


WIDE = 3 * PAD + 384


def pack_kernel(gu_ref, down_ref, qkv_ref, gains_ref, order_ref, *refs):
    outs, held, extra = refs[:8], refs[8], refs[9]
    keep = lax.broadcasted_iota(jnp.int32, (8, PAD), 1) < UNITS
    for part, (ref, base) in enumerate(((gu_ref, 0), (gu_ref, FF), (down_ref, 0))):
        for p in range(4):
            at = base + 2 * UNITS * p
            both = ref[:, at : at + 2 * UNITS].astype(F32)
            turned = pltpu.roll(both, UNITS, 1)
            held[2 * p, :, PAD * part : PAD * part + PAD] = jnp.where(keep, both[:, :PAD], 0.0)
            held[2 * p + 1, :, PAD * part : PAD * part + PAD] = jnp.where(keep, turned[:, :PAD], 0.0)
    extra[...] = jnp.zeros_like(extra)
    extra[0:1, 0:17] = gains_ref[...].astype(F32)
    extra[1:2, 0:32] = order_ref[...].astype(F32)
    low = lanes_of(8) < 64
    at = 3 * PAD
    for j in range(8):
        held[j, :, at : at + 128] = qkv_ref[:, 128 * j : 128 * j + 128].astype(F32)
        k = qkv_ref[:, 1024 + 128 * (j // 2) : 1152 + 128 * (j // 2)].astype(F32)
        v = qkv_ref[:, 1536 + 128 * (j // 2) : 1664 + 128 * (j // 2)].astype(F32)
        if j % 2:
            k = pltpu.roll(k, 64, 1)
        else:
            v = pltpu.roll(v, 64, 1)
        held[j, :, at + 128 : at + 256] = jnp.where(low, k, v)
        held[j, :, at + 256 : at + 384] = extra[...]
    for r in range(8):
        outs[r][...] = held[sequence_of(r)].astype(BF)


def pack(w_gu, w_down, w_qkv, gains, order):
    return pl.pallas_call(
        pack_kernel,
        out_shape=[shape((8, WIDE))] * 8,
        in_specs=[VMEM] * 5,
        out_specs=[VMEM] * 8,
        scratch_shapes=[pltpu.VMEM((8, 8, WIDE), F32), pltpu.VMEM((8, 128), F32)],
        compiler_params=params(16),
        cost_estimate=slow(10**9),
    )(w_gu, w_down, w_qkv, gains, order)


def merge_kernel(*refs):
    wout_ref, ff_ref, seq_ref, held = refs[9:]
    for c in range(8):
        held[144 + 8 * c : 152 + 8 * c, :] = wout_ref[:, 128 * c : 128 * c + 128].astype(F32)
    at = 3 * PAD
    for r in range(8):
        j = sender_of(r)
        got = refs[r][...]
        ff_ref[j] = got[:, :at]
        rest = got[:, at:].astype(F32)
        row = pl.multiple_of(8 * j, 8)
        held[pl.ds(row, 8), :] = rest[:, :128]
        held[pl.ds(row + 64, 8), :] = rest[:, 128:256]
        held[pl.ds(128 + j, 1), :] = rest[0:1, 256:]
        held[pl.ds(136 + j, 1), :] = rest[1:2, 256:]
    for s in range(16):
        seq_ref[s] = held[...].astype(BF)


def merge(blocks, wait, w_out):
    return pl.pallas_call(
        merge_kernel,
        out_shape=[shape((8, 8, 3 * PAD)), shape((16, 208, 128))],
        in_specs=[VMEM] * 8 + [ANY, VMEM],
        out_specs=[VMEM] * 2,
        scratch_shapes=[pltpu.VMEM((208, 128), F32)],
        compiler_params=params(16),
        cost_estimate=slow(10**9),
    )(*blocks, wait, w_out)


def part_kernel(g_ref, *outs):
    for r in range(8):
        outs[r][...] = g_ref[sequence_of(r)]


def part(g):
    return pl.pallas_call(
        part_kernel,
        out_shape=[shape((8, 3 * PAD))] * 8,
        in_specs=[VMEM],
        out_specs=[VMEM] * 8,
        compiler_params=params(16),
        cost_estimate=slow(10**9),
    )(g)


def unpack_kernel(*refs):
    gu_ref, down_ref, held = refs[8:]
    for r in range(8):
        held[sender_of(r)] = refs[r][...].astype(F32)
    first = lax.broadcasted_iota(jnp.int32, (8, 2 * UNITS), 1) < UNITS
    blank = jnp.zeros((8, 2 * UNITS - PAD), F32)
    for k, (ref, base) in enumerate(((gu_ref, 0), (gu_ref, FF), (down_ref, 0))):
        for p in range(4):
            a, b = [
                jnp.concatenate([held[2 * p + i, :, PAD * k : PAD * k + PAD], blank], axis=1)
                for i in range(2)
            ]
            at = base + 2 * UNITS * p
            ref[:, at : at + 2 * UNITS] = jnp.where(first, a, pltpu.roll(b, UNITS, 1))


def unpack(blocks):
    return pl.pallas_call(
        unpack_kernel,
        out_shape=[shape((8, 2 * FF), F32), shape((8, FF), F32)],
        in_specs=[VMEM] * 8,
        out_specs=[VMEM] * 2,
        scratch_shapes=[pltpu.VMEM((8, 8, 3 * PAD), F32)],
        compiler_params=params(16),
        cost_estimate=pl.CostEstimate(flops=0, bytes_accessed=1 << 20, transcendentals=0),
    )(*blocks)


def lanes_of(rows):
    return lax.broadcasted_iota(jnp.int32, (rows, 128), 1)


def head_mean(v, lane):
    low = jnp.sum(jnp.where(lane < 64, v, 0.0), axis=-1, keepdims=True)
    high = jnp.sum(jnp.where(lane < 64, 0.0, v), axis=-1, keepdims=True)
    return jnp.where(lane < 64, low, high) * (1.0 / HD)


def partner(v, lane):
    return jnp.where((lane & 32) == 0, pltpu.roll(v, 96, 1), pltpu.roll(v, 32, 1))


def trig(tables, orders_ref, b):
    cf, sf, cn, sn = tables
    s = lax.axis_index(SEQ)
    sign = jnp.where((lanes_of(SPAN) & 32) == 0, -1.0, 1.0)
    cos, sin = [], []
    for k in range(2):
        span = orders_ref[b, 2 * s + k]
        c, d = cf[pl.ds(span, 1), :], sf[pl.ds(span, 1), :]
        cos.append(c * cn[...] - d * sn[...])
        sin.append((d * cn[...] + c * sn[...]) * sign)
    return jnp.concatenate(cos), jnp.concatenate(sin)


def project_kernel(*refs):
    toks = refs[:8]
    got_ref, a_gain, qk_gain, orders_ref = refs[8:12]
    tables = refs[12:16]
    send_ref, x_ref, h_ref, mixed_ref, w_ref, wout_ref, w32, wout32 = refs[16:]
    step = pl.program_id(0)

    @pl.when(step == 0)
    def _():
        for s in range(16):
            got = got_ref[s, 0:208, :].astype(F32)
            for j in range(8):
                at = 128 * j + 8 * s
                w32[at : at + 8, :128] = got[8 * j : 8 * j + 8]
                w32[at : at + 8, 128:] = got[64 + 8 * j : 72 + 8 * j]
                wout32[8 * s : 8 * s + 8, 128 * j : 128 * j + 128] = got[144 + 8 * j : 152 + 8 * j]
        w_ref[...] = w32[...].astype(BF)
        wout_ref[...] = wout32[...].astype(BF)

    lane = lanes_of(128)
    low = lane < 64
    def sequence(r):
        x = toks[r][...]
        at = slice(128 * (r % 2), 128 * (r % 2) + 128)
        x_ref[at, :] = x
        x = x.astype(F32)
        h = (x * inv_rms(x) * a_gain[...]).astype(BF)
        h_ref[at, :] = h
        mixed = mm(h, w_ref[...])
        mixed_ref[at, :] = mixed
        b = sequence_of(r)
        cos, sin = trig(tables, orders_ref, b)

        def turned(v, gain):
            g = v * lax.rsqrt(head_mean(v * v, lane) + EPSILON) * gain
            return g * cos + partner(g, lane) * sin

        q = turned(mixed[:, :128], qk_gain[0:1, :])
        kv = jnp.where(low, turned(mixed[:, 128:], qk_gain[1:2, :]), mixed[:, 128:]).astype(BF)
        flip = pltpu.roll(q, 64, 1)
        l64 = low[:64]
        send_ref[2 * b, 0:128, :] = kv
        send_ref[2 * b + 1, 0:128, :] = kv
        send_ref[2 * b, 128:192, :] = jnp.where(l64, q[:64], flip[64:]).astype(BF)
        send_ref[2 * b + 1, 128:192, :] = jnp.where(l64, flip[:64], q[64:]).astype(BF)

    for o in range(4):

        @pl.when(step == o)
        def _():
            sequence(2 * o)
            sequence(2 * o + 1)


def project(toks, got, a_gain, qk_gain, orders, tables):
    return pl.pallas_call(
        project_kernel,
        out_shape=[
            shape((16, 192, 128)),
            shape((1024, 1024)),
            shape((1024, 1024)),
            shape((1024, 256), F32),
            shape((1024, 256)),
            shape((128, 1024)),
        ],
        grid=(4,),
        in_specs=[whole(128, 1024)] * 8
        + [whole(16, 208, 128), whole(1, 1024), whole(2, 128), SMEM]
        + [whole(SPANS, 128)] * 2
        + [whole(SPAN, 128)] * 2,
        out_specs=[
            whole(16, 192, 128),
            rows(256, 1024),
            rows(256, 1024),
            rows(256, 256),
            whole(1024, 256),
            whole(128, 1024),
        ],
        scratch_shapes=[pltpu.VMEM((1024, 256), F32), pltpu.VMEM((128, 1024), F32)],
        compiler_params=params(40),
        cost_estimate=slow(10**11),
    )(*toks, got, a_gain, qk_gain, orders, *tables)


def attend_kernel(qkv_ref, orders_ref, send_ref, q_ref, kv_ref, ot_ref, lse_ref, kvt, osc):
    b = lax.axis_index(SEQ) // 2
    l64 = lanes_of(64) < 64
    for i in range(32):
        at = pl.multiple_of(orders_ref[b, i] * 64, 64)
        kv_ref[pl.ds(at, 64), :] = qkv_ref[i // 2, 64 * (i % 2) : 64 * (i % 2) + 64, :]
        block = qkv_ref[i // 2, 128:192, :].astype(F32)
        if i % 2:
            block = pltpu.roll(block, 64, 1)
        q_ref[pl.ds(at, 64), :] = jnp.where(l64, block * HD**-0.5, 0.0).astype(BF)
    kvt[...] = kv_ref[...].T
    after = lax.broadcasted_iota(jnp.int32, (256, 256), 0) > lax.broadcasted_iota(
        jnp.int32, (256, 256), 1
    )
    for i in range(8):
        n = 256 * i
        q = q_ref[n : n + 256, :]
        near = jnp.where(after, -1e30, mm(kv_ref[n : n + 256, :], q, 1, 1))
        top = jnp.max(near, axis=0, keepdims=True)
        if i:
            far = mm(kv_ref[:n, :], q, 1, 1)
            top = jnp.maximum(top, jnp.max(far, axis=0, keepdims=True))
        near = jnp.exp(near - top)
        total = jnp.sum(near, axis=0, keepdims=True)
        o = mm(kvt[:, n : n + 256], near.astype(BF))
        if i:
            far = jnp.exp(far - top)
            total = total + jnp.sum(far, axis=0, keepdims=True)
            o = o + mm(kvt[:, :n], far.astype(BF))
        o = o / total
        ot_ref[:, n : n + 256] = o[64:]
        lse_ref[:, n : n + 256] = top + jnp.log(total)
        osc[n : n + 256, :] = o.T
    for i in range(16):
        a = osc[pl.ds(pl.multiple_of(orders_ref[b, 2 * i] * 64, 64), 64), :]
        c = osc[pl.ds(pl.multiple_of(orders_ref[b, 2 * i + 1] * 64, 64), 64), :]
        send_ref[i] = jnp.where(l64, pltpu.roll(a, 64, 1), c).astype(BF)


def attend(qkv, orders):
    return pl.pallas_call(
        attend_kernel,
        out_shape=[
            shape((16, 64, 128)),
            shape((2048, 128)),
            shape((2048, 128)),
            shape((64, 2048), F32),
            shape((1, 2048), F32),
        ],
        in_specs=[VMEM, SMEM],
        out_specs=[VMEM] * 5,
        scratch_shapes=[pltpu.VMEM((128, 2048), BF), pltpu.VMEM((2048, 128), F32)],
        compiler_params=params(40),
        cost_estimate=pl.CostEstimate(flops=2 * 2048 * 2048 * 128, bytes_accessed=4 << 20, transcendentals=2 << 20),
    )(qkv, orders)


def attend_back_kernel(
    got_ref, q_ref, kv_ref, ot_ref, lse_ref, orders_ref, send_ref, do, kvt, dkv, dqs
):
    b = lax.axis_index(SEQ) // 2
    l64 = lanes_of(64) < 64
    for i in range(32):
        at = pl.multiple_of(orders_ref[b, i] * 64, 64)
        block = got_ref[i // 2].astype(F32)
        if i % 2 == 0:
            block = pltpu.roll(block, 64, 1)
        do[pl.ds(at, 64), :] = jnp.where(l64, 0.0, block)
    kvt[...] = kv_ref[...].T
    before = lax.broadcasted_iota(jnp.int32, (256, 256), 0) <= lax.broadcasted_iota(
        jnp.int32, (256, 256), 1
    )
    dkv[...] = jnp.zeros_like(dkv)
    for i in range(8):
        n = 256 * i
        q = q_ref[n : n + 256, :]
        d32 = do[n : n + 256, :]
        d = d32.astype(BF)
        lse = lse_ref[:, n : n + 256]
        delta = jnp.sum(ot_ref[:, n : n + 256] * d32.T[64:], axis=0, keepdims=True)
        dq = None
        for lo, hi in ((n, n + 256), (0, n)):
            if lo == hi:
                continue
            keys = kv_ref[lo:hi, :]
            p = jnp.exp(mm(keys, q, 1, 1) - lse)
            if lo:
                p = jnp.where(before, p, 0.0)
            elif hi == 256 and n == 0:
                p = jnp.where(before, p, 0.0)
            ds = (p * (mm(keys, d, 1, 1) - delta)).astype(BF)
            dkv[lo:hi, :] += mm(ds, q) + mm(p.astype(BF), d)
            term = mm(kvt[:, lo:hi], ds)
            dq = term if dq is None else dq + term
        dqs[n : n + 256, :] = (dq * HD**-0.5).T
    for i in range(16):
        at = pl.multiple_of(orders_ref[b, 2 * i] * 64, 64)
        bt = pl.multiple_of(orders_ref[b, 2 * i + 1] * 64, 64)
        send_ref[i, 0:64, :] = dkv[pl.ds(at, 64), :].astype(BF)
        send_ref[i, 64:128, :] = dkv[pl.ds(bt, 64), :].astype(BF)
        send_ref[i, 128:192, :] = jnp.where(
            l64, dqs[pl.ds(at, 64), :], pltpu.roll(dqs[pl.ds(bt, 64), :], 64, 1)
        ).astype(BF)


def attend_back(got, q, kv, ot, lse, orders):
    return pl.pallas_call(
        attend_back_kernel,
        out_shape=shape((16, 192, 128)),
        in_specs=[VMEM] * 5 + [SMEM],
        out_specs=VMEM,
        scratch_shapes=[
            pltpu.VMEM((2048, 128), F32),
            pltpu.VMEM((128, 2048), BF),
            pltpu.VMEM((2048, 128), F32),
            pltpu.VMEM((2048, 128), F32),
        ],
        compiler_params=params(40),
        cost_estimate=pl.CostEstimate(flops=5 * 2048 * 2048 * 128, bytes_accessed=4 << 20, transcendentals=2 << 20),
    )(got, q, kv, ot, lse, orders)


def heads_of(pair, r):
    l64 = lanes_of(64) < 64
    b = sequence_of(r)
    a = pair[2 * b].astype(F32)
    c = pair[2 * b + 1].astype(F32)
    return jnp.concatenate(
        [jnp.where(l64, a, pltpu.roll(c, 64, 1)), jnp.where(l64, pltpu.roll(a, 64, 1), c)]
    )


def feed_kernel(*refs):
    douts, atn, wouts = refs[:8], refs[8:16], refs[16:24]
    x_ref, f_gain, w_ref = refs[24:27]
    keep_ref, give_ref, x1_ref, h2_ref, act_ref, dgu_ref, gf_ref, wo = refs[27:]
    step = pl.program_id(0)

    @pl.when(step == 0)
    def _():
        for r in range(8):
            wo[128 * r : 128 * r + 128, :] = wouts[r][...]
        gf_ref[...] = jnp.zeros_like(gf_ref)

    def block(o):
        cols = [
            jnp.concatenate([heads_of(atn[k], 4 * o + i) for i in range(4)]).astype(BF)
            for k in range(8)
        ]
        attn = jnp.concatenate(cols, axis=1)
        x1 = x_ref[...].astype(F32) + mm(attn, wo[...])
        if o == 0:
            x1_ref[...] = x1[:128]
        n2 = x1 * inv_rms(x1)
        h2 = (n2 * f_gain[...]).astype(BF)
        h2_ref[...] = h2
        gate_up = mm(h2, w_ref[:, : 2 * PAD])
        gate, upper = gate_up[:, :PAD], gate_up[:, PAD:]
        sigma = jax.nn.sigmoid(gate)
        swish = gate * sigma
        act_ref[...] = (swish * upper).astype(BF)
        d = jnp.concatenate([douts[4 * o + i][...] for i in range(4)])
        d_act = mm(d, w_ref[:, 2 * PAD :]).astype(BF).astype(F32)
        d_gate = d_act * upper * (sigma * (1.0 + gate * (1.0 - sigma)))
        dgu_ref[:, :PAD] = d_gate.astype(BF)
        dgu_ref[:, PAD:] = (d_act * swish).astype(BF)
        d_h2 = mm(dgu_ref[...], w_ref[:, : 2 * PAD], 1, 1)
        gf_ref[...] += jnp.sum(d_h2 * n2, axis=0, keepdims=True)
        for i in range(2):
            keep_ref[i] = d_h2[256 * i : 256 * i + 128].astype(BF)
            give_ref[i] = d_h2[256 * i + 128 : 256 * i + 256].astype(BF)

    for o in range(2):
        pl.when(step == o)(lambda o=o: block(o))


QUARTER = pl.BlockSpec((1, 128, 1024), lambda i: (i, 0, 0))
HALF = pl.BlockSpec((2, 128, 1024), lambda i: (i, 0, 0))


def feed(douts, attns, wouts, x, f_gain, w_ff):
    return pl.pallas_call(
        feed_kernel,
        out_shape=[
            near((4, 128, 1024)),
            shape((4, 128, 1024)),
            shape((128, 1024), F32),
            shape((1024, 1024)),
            shape((1024, PAD)),
            shape((1024, 2 * PAD)),
            shape((1, 1024), F32),
        ],
        grid=(2,),
        in_specs=[whole(128, 1024)] * 8
        + [whole(16, 64, 128)] * 8
        + [whole(128, 1024)] * 8
        + [rows(512, 1024), whole(1, 1024), whole(1024, 3 * PAD)],
        out_specs=[
            HALF,
            HALF,
            whole(128, 1024),
            rows(512, 1024),
            rows(512, PAD),
            rows(512, 2 * PAD),
            whole(1, 1024),
        ],
        scratch_shapes=[pltpu.VMEM((1024, 1024), BF)],
        compiler_params=params(56),
        cost_estimate=pl.CostEstimate(flops=2 * 1024 * 1024 * 4224, bytes_accessed=20 << 20, transcendentals=1 << 20),
    )(*douts, *attns, *wouts, x, f_gain, w_ff)


def feed_grad_kernel(*refs):
    douts = refs[:8]
    h2_ref, act_ref, dgu_ref, w_ref = refs[8:12]
    g_ref, keep_ref, give_ref, ht, dt = refs[12:]
    for r in range(8):
        dt[:, 128 * r : 128 * r + 128] = douts[r][...].T
    ht[...] = h2_ref[...].T
    for p in range(4):
        for n, part_of in enumerate(((ht, dgu_ref), (dt, act_ref))):
            left, right = part_of
            at = slice(2 * PAD * n, 2 * PAD * n + right.shape[1])
            g = mm(left[256 * p : 256 * p + 256, :], right[...])
            for s in range(16):
                pair = [g[8 * s : 8 * s + 8], g[128 + 8 * s : 136 + 8 * s]]
                g_ref[s, 16 * p : 16 * p + 16, at] = jnp.concatenate(pair).astype(BF)
    for o in range(4):
        out = mm(act_ref[256 * o : 256 * o + 256, :], w_ref[...], 1, 1)
        keep_ref[o] = out[:128].astype(BF)
        give_ref[o] = out[128:].astype(BF)


def feed_grad(douts, h2, act, d_gu, w_ff):
    return pl.pallas_call(
        feed_grad_kernel,
        out_shape=[shape((16, 64, 3 * PAD)), near((4, 128, 1024)), shape((4, 128, 1024))],
        grid=(1,),
        in_specs=[whole(128, 1024)] * 8
        + [whole(1024, 1024), whole(1024, PAD), whole(1024, 2 * PAD)]
        + [pl.BlockSpec((1024, PAD), lambda i: (0, 2))],
        out_specs=[whole(16, 64, 3 * PAD), whole(4, 128, 1024), whole(4, 128, 1024)],
        scratch_shapes=[pltpu.VMEM((1024, 1024), BF), pltpu.VMEM((1024, 1024), BF)],
        compiler_params=params(56),
        cost_estimate=pl.CostEstimate(flops=2 * 1024 * 1024 * 2560, bytes_accessed=18 << 20, transcendentals=0),
    )(*douts, h2, act, d_gu, w_ff)


def unproject_kernel(*refs):
    x_ref, back_ref, mixed_ref, w_ref, qk_gain, orders_ref = refs[:6]
    tables = refs[6:10]
    keep_ref, give_ref, dm_ref, ga_ref, gqk_ref = refs[10:]
    lane = lanes_of(128)
    low = lane < 64
    step = pl.program_id(0)

    @pl.when(step == 0)
    def _():
        ga_ref[...] = jnp.zeros_like(ga_ref)
        gqk_ref[...] = jnp.zeros_like(gqk_ref)

    def sequence(r):
        b = sequence_of(r)
        cos, sin = trig(tables, orders_ref, b)
        at = slice(128 * (r % 2), 128 * (r % 2) + 128)
        mixed = mixed_ref[at, :]
        u = back_ref[2 * b].astype(F32)
        v = back_ref[2 * b + 1].astype(F32)
        d_kv = u[:128] + v[:128]
        u, v = u[128:], v[128:]
        l64 = low[:64]
        d_q = jnp.concatenate(
            [
                jnp.where(l64, u, pltpu.roll(v, 64, 1)),
                jnp.where(l64, pltpu.roll(u, 64, 1), v),
            ]
        )

        def turned_back(d, raw, gain):
            scale = lax.rsqrt(head_mean(raw * raw, lane) + EPSILON)
            unit = raw * scale
            g = d * cos - partner(d, lane) * sin
            e = g * gain
            grad = jnp.sum(g * unit, axis=0, keepdims=True)
            return scale * (e - unit * head_mean(e * unit, lane)), grad

        dq_raw, grad_q = turned_back(d_q, mixed[:, :128], qk_gain[0:1, :])
        dk_raw, grad_k = turned_back(d_kv, mixed[:, 128:], qk_gain[1:2, :])
        gqk_ref[0:1, :] += grad_q
        gqk_ref[1:2, :] += grad_k
        dm = jnp.concatenate([dq_raw, jnp.where(low, dk_raw, d_kv)], axis=1).astype(BF)
        dm_ref[at, :] = dm
        d_h = mm(dm, w_ref[...], 1, 1)
        x = x_ref[at, :].astype(F32)
        ga_ref[...] += jnp.sum(d_h * (x * inv_rms(x)), axis=0, keepdims=True)
        (give_ref if r % 2 else keep_ref)[0] = d_h.astype(BF)

    for o in range(4):

        @pl.when(step == o)
        def _():
            sequence(2 * o)
            sequence(2 * o + 1)


def unproject(x, back, mixed, w, qk_gain, orders, tables):
    return pl.pallas_call(
        unproject_kernel,
        out_shape=[
            near((4, 128, 1024)),
            shape((4, 128, 1024)),
            shape((1024, 256)),
            shape((1, 1024), F32),
            shape((2, 128), F32),
        ],
        grid=(4,),
        in_specs=[
            rows(256, 1024),
            whole(16, 192, 128),
            rows(256, 256),
            whole(1024, 256),
            whole(2, 128),
            SMEM,
        ]
        + [whole(SPANS, 128)] * 2
        + [whole(SPAN, 128)] * 2,
        out_specs=[QUARTER, QUARTER, rows(256, 256), whole(1, 1024), whole(2, 128)],
        compiler_params=params(40),
        cost_estimate=pl.CostEstimate(flops=2 * 1024 * 1024 * 256, bytes_accessed=8 << 20, transcendentals=0),
    )(far(x), back, far(mixed), far(w), qk_gain, orders, *tables)


def own_kernel(t0, t1, t2, t3, x1_ref, f_gain, d_ref, *refs):
    wouts, dx_ref, send_ref = refs[:8], refs[8], refs[9]
    d_h2 = sum(t[...].astype(F32) for t in (t0, t1, t2, t3))
    x1 = x1_ref[...]
    scale = inv_rms(x1)
    d_x1 = d_ref[...].astype(F32) + rms_back(d_h2, x1 * scale, scale, f_gain[...])
    dx_ref[...] = d_x1
    branch = d_x1.astype(BF)
    for j in range(8):
        send_ref[j, 128:256, :] = branch[:, 128 * j : 128 * j + 128]
    l64 = lanes_of(64) < 64
    for k in range(8):
        j = sequence_of(k)
        d_attn = mm(branch, wouts[k][...], 1, 1)
        top, low = d_attn[:64], d_attn[64:]
        send_ref[j, 0:64, :] = jnp.where(l64, top, pltpu.roll(low, 64, 1)).astype(BF)
        send_ref[j, 64:128, :] = jnp.where(l64, pltpu.roll(top, 64, 1), low).astype(BF)


def own_tokens(terms, x1, f_gain, d_out, wouts):
    return pl.pallas_call(
        own_kernel,
        out_shape=[shape((128, 1024), F32), shape((8, 256, 128))],
        in_specs=[VMEM] * 15,
        out_specs=[VMEM] * 2,
        compiler_params=params(32),
        cost_estimate=slow(10**11),
    )(*terms, x1, f_gain, d_out, *wouts)


def out_grad_kernel(*refs):
    atn, got_ref, h_ref, out_ref, ht_ref = refs[:8], *refs[8:]
    ht_ref[...] = h_ref[...].T
    d = jnp.concatenate([got_ref[sequence_of(r), 128:256, :] for r in range(8)])
    for k in range(8):
        attn = jnp.concatenate([heads_of(atn[k], r) for r in range(8)])
        grad = mm(attn.T.astype(BF), d)
        out_ref[pl.ds(16 * sequence_of(k), 16)] = grad.reshape(16, 8, 128)


def out_grad(attns, got, h):
    return pl.pallas_call(
        out_grad_kernel,
        out_shape=[shape((128, 8, 128), F32), shape((1024, 1024))],
        in_specs=[VMEM] * 10,
        out_specs=[VMEM] * 2,
        compiler_params=params(32),
        cost_estimate=pl.CostEstimate(flops=2 * 128 * 1024 * 1024, bytes_accessed=3 << 20, transcendentals=0),
    )(*attns, got, h)


def last_kernel(ht_ref, dm_ref, gout_ref, gains_ref, out_ref):
    g = mm(ht_ref[...], dm_ref[...])
    a = g[:, :128].reshape(128, 8, 128)
    b = g[:, 128:].reshape(128, 8, 128)
    out_ref[:, 0:16, :] = jnp.concatenate([a, b], axis=1).astype(BF)
    out_ref[:, 16:32, :] = jnp.concatenate([gout_ref[...], gains_ref[...]], axis=1).astype(BF)


def last_pack(h, d_mixed, g_out, gains):
    return pl.pallas_call(
        last_kernel,
        out_shape=shape((128, 32, 128)),
        in_specs=[VMEM] * 4,
        out_specs=VMEM,
        compiler_params=params(32),
        cost_estimate=slow(10**9),
    )(far(h), far(d_mixed), g_out, gains)


def finish_kernel(last_ref, t0, t1, t2, t3, x_ref, a_gain, dx_ref, dtok_ref, gqkv_ref, gout_ref, gains_ref):
    d_h = sum(t[...].astype(F32) for t in (t0, t1, t2, t3))
    x = x_ref[...].astype(F32)
    scale = inv_rms(x)
    dtok_ref[...] = dx_ref[...] + rms_back(d_h, x * scale, scale, a_gain[...])
    low = lanes_of(8) < 64
    gains = jnp.zeros((8, 128), F32)
    for p in range(4):
        kv = []
        for j in (2 * p, 2 * p + 1):
            acc = jnp.sum(last_ref[16 * j : 16 * j + 16].astype(F32), axis=0)
            gqkv_ref[:, 128 * j : 128 * j + 128] = acc[0:8]
            kv.append(acc[8:16])
            gout_ref[:, 128 * j : 128 * j + 128] = acc[16:24]
            gains = gains + acc[24:32]
        at = 1024 + 128 * p
        gqkv_ref[:, at : at + 128] = jnp.where(low, kv[0], pltpu.roll(kv[1], 64, 1))
        gqkv_ref[:, at + 512 : at + 640] = jnp.where(low, pltpu.roll(kv[0], 64, 1), kv[1])
    gains_ref[...] = gains + pltpu.roll(gains, 128 - 17, 1)


def finish(last, terms, x, a_gain, d_x1):
    return pl.pallas_call(
        finish_kernel,
        out_shape=[
            shape((128, 1024), F32),
            shape((8, 2048), F32),
            shape((8, 1024), F32),
            shape((8, 128), F32),
        ],
        in_specs=[VMEM] * 8,
        out_specs=[VMEM] * 4,
        compiler_params=params(32),
        cost_estimate=slow(10**9),
    )(last, *terms, x, a_gain, d_x1)


def on_device(tokens, w_qkv, w_out, w_gu, w_down, gains, span_order, d_out):
    tables = [jnp.asarray(a) for a in lane_tables()]

    toks = gather_dp(tokens[0])
    packed = pack(far(w_gu), far(w_down), far(w_qkv), gains[None], span_order)
    ff_pay, seq_pay = merge(trade(packed), toks[4], w_out)
    got = swap_all(seq_pay, SEQ)
    w_ff = lax.all_gather(ff_pay, SEQ, axis=1, tiled=False).reshape(1024, 3 * PAD)

    gain_all = got[:, 128:136, :17].transpose(1, 0, 2).reshape(2176).astype(F32)
    orders = got[0, 136:144, :32].astype(jnp.int32)
    a_gain = gain_all[None, :1024]
    f_gain = gain_all[None, 1024:2048]
    q_gain, k_gain = gain_all[2048:2112], gain_all[2112:]
    qk_gain = jnp.stack([jnp.concatenate([q_gain, q_gain]), jnp.concatenate([k_gain, k_gain])])

    send, x_all, h, mixed, w_j, w_out_j = project(toks, got, a_gain, qk_gain, orders, tables)
    qkv = swap_all(send, SEQ)
    douts = gather_dp(d_out[0])
    o_send, q_s, kv_s, ot, lse = attend(qkv, orders)
    wouts = gather_dp(w_out_j)
    o_got = swap_all(o_send, SEQ)
    attns = gather_dp(o_got)
    d_keep, d_give, x1, h2, act, d_gu, gf_part = feed(
        douts, attns, wouts, x_all, f_gain, w_ff
    )
    s_h2 = halve(d_keep, d_give)
    h2, *s_h2 = lax.optimization_barrier((h2, *s_h2))
    d_x1, d_send = own_tokens(exchange(s_h2), x1, f_gain, d_out[0], wouts)

    g_ff, out_keep, out_give = feed_grad(douts, h2, act, d_gu, w_ff)
    g_ff = lax.psum_scatter(g_ff.reshape(1024, 3 * PAD), SEQ, scatter_dimension=0, tiled=True)

    d_got = swap_all(d_send, DP)
    d_o = swap_all(d_got[:, :128].reshape(16, 64, 128), SEQ)
    d_o, out_keep, out_give = lax.optimization_barrier((d_o, out_keep, out_give))
    terms = exchange(halve(out_keep, out_give))
    back = swap_all(attend_back(d_o, q_s, kv_s, ot, lse, orders), SEQ)
    g_out_part, h_turned = out_grad(attns, d_got, h)
    back, terms, g_out_part = lax.optimization_barrier((back, terms, g_out_part))
    result = x1 + total_of(terms)
    h_keep, h_give, d_mixed, ga_part, gqk_part = unproject(
        x_all, back, mixed, w_j, qk_gain, orders, tables
    )
    s_h = halve(h_keep, h_give)
    gq_part = gqk_part[0, :64] + gqk_part[0, 64:]
    g_gain = jnp.concatenate([ga_part[0], gf_part[0], gq_part, gqk_part[1, :64]]).reshape(128, 17)
    gain_hi = g_gain.astype(BF).astype(F32)
    gain_rows = jnp.concatenate([gain_hi, g_gain - gain_hi, jnp.zeros((128, 94), F32)], axis=1)
    gain_rows = jnp.broadcast_to(gain_rows[:, None], (128, 8, 128))
    gain_rows, *s_h = lax.optimization_barrier((gain_rows, *s_h))
    h_terms = exchange(s_h)
    last = swap_all(last_pack(h_turned, d_mixed, g_out_part, gain_rows), ALL)
    g_gu, g_down = unpack(trade(part(g_ff.reshape(8, 8, 3 * PAD))))
    last, g_gu, g_down, *h_terms = lax.optimization_barrier((last, g_gu, g_down, *h_terms))
    d_tokens, g_qkv, g_out, g_gains = finish(last, h_terms, tokens[0], a_gain, d_x1)
    return (
        result.astype(BF)[None],
        d_tokens[None],
        g_qkv,
        g_out,
        g_gu,
        g_down,
        g_gains[0, :17],
    )


def solution(mesh):
    split = Mesh(mesh.devices.reshape(4, 2, 4, 4), ALL)
    return jax.shard_map(
        on_device,
        mesh=split,
        in_specs=(
            P(DP, SEQ, None),
            P(ALL, None),
            P(ALL, None),
            P(ALL, None),
            P(ALL, None),
            P(ALL),
            P(DP, None),
            P(DP, SEQ, None),
        ),
        out_specs=(
            P(DP, SEQ, None),
            P(DP, SEQ, None),
            P(ALL, None),
            P(ALL, None),
            P(ALL, None),
            P(ALL, None),
            P(ALL),
        ),
        check_vma=False,
    )
```
